256 devices in a mesh: ctx: 32 (over z, x_lo, core), head: 8 (over y, x_hi).
Axes of the slice: x: 4 (x_hi: 2, x_lo: 2; x = x_hi * 2 + x_lo), y: 4, z: 8, core: 2. Of those that a mesh axis runs over, the one named last changes fastest.
Arguments:
- vid_query: bfloat16 [32, 8192, 128], P('head', 'ctx')
- vid_key: bfloat16 [32, 8192, 128], P('head', 'ctx')
- vid_value: bfloat16 [32, 8192, 128], P('head', 'ctx'), may hold values from -6 to 6
- vid_out: bfloat16 [32, 8192, 128], P('head', 'ctx'), may hold values from -6 to 6
- vid_grad: bfloat16 [32, 8192, 128], P('head', 'ctx'), may hold values from -96 to 96
- vid_lse: float32 [32, 8192], P('head', 'ctx'), as said below
- vid_mask: int32 [32, 8192, 256], P('head', 'ctx'), may hold values from 0 to 255
- aud_query: bfloat16 [32, 2048, 128], P('head', 'ctx')
- aud_key: bfloat16 [32, 2048, 128], P('head', 'ctx')
- aud_value: bfloat16 [32, 2048, 128], P('head', 'ctx'), may hold values from -6 to 6
- aud_out: bfloat16 [32, 2048, 128], P('head', 'ctx'), may hold values from -6 to 6
- aud_grad: bfloat16 [32, 2048, 128], P('head', 'ctx'), may hold values from -384 to 384
- aud_lse: float32 [32, 2048], P('head', 'ctx'), as said below
- aud_mask: int32 [32, 2048, 1024], P('head', None, 'ctx'), may hold values from 0 to 255
- gain_vq: float32 [32, 128], P('head'), may hold values from 0.5 to 1.5
- gain_ak: float32 [32, 128], P('head'), may hold values from 0.5 to 1.5
- gain_aq: float32 [32, 128], P('head'), may hold values from 0.5 to 1.5
- gain_vk: float32 [32, 128], P('head'), may hold values from 0.5 to 1.5
Outputs:
- grad_vid_query: bfloat16 [32, 8192, 128], P('head', 'ctx')
- grad_vid_key: bfloat16 [32, 8192, 128], P('head', 'ctx')
- grad_vid_value: bfloat16 [32, 8192, 128], P('head', 'ctx')
- grad_aud_query: bfloat16 [32, 2048, 128], P('head', 'ctx')
- grad_aud_key: bfloat16 [32, 2048, 128], P('head', 'ctx')
- grad_aud_value: bfloat16 [32, 2048, 128], P('head', 'ctx')
The draws below stay inside these ranges and needn't reach their ends.
Inputs may be any that keep to these rules, and one draw needn't show every extreme that they name: `vid_lse`: every entry lies between ln(2048) and ln(2048) + 1.5. `aud_lse`: every entry lies between ln(8192) and ln(8192) + 1.5.
All inputs are finite; a program needn't handle non-finite values.
Results may differ from the reference program's by a relative error of at most 0.011.
Values may be sent and summed in bfloat16 or wider, within the bound.
No kernel may reach another device: no remote copies, remote signals or barrier semaphores. Data moves between devices by JAX's collectives and lax.ppermute only.
A program may use at most 128 MiB of HBM per device.

```python
import math
import jax
import jax.numpy as jnp
from jax import lax

DH = 128
HEADS = 32
VIDEO = 8192
AUDIO = 2048


def token_field(seed_key, row_count, head_rise):
    base_key, row_key, column_key = jax.random.split(seed_key, 3)
    field_shape = (HEADS, row_count, DH)
    normal_values = jax.random.normal(base_key, field_shape, jnp.float32)
    base_values = normal_values
    row_scale = jnp.exp(jax.random.uniform(row_key, (1, row_count, 1), jnp.float32, math.log(0.3), math.log(3.0)))
    column_scale = jnp.exp(jax.random.uniform(column_key, (HEADS, 1, DH), jnp.float32, math.log(0.5), math.log(2.0)))
    head_scale = head_rise ** (jnp.arange(HEADS, dtype=jnp.float32) / max(HEADS - 1, 1))
    return (base_values * row_scale * column_scale * head_scale[:, None, None]).astype(jnp.bfloat16)


def draw_vid_query(key, part):
    key = jax.random.fold_in(key, 11)
    return token_field(key, VIDEO, 1.5)


def draw_vid_key(key, part):
    key = jax.random.fold_in(key, 12)
    return token_field(key, VIDEO, 1.5)


def draw_aud_query(key, part):
    key = jax.random.fold_in(key, 13)
    return token_field(key, AUDIO, 1.5)


def draw_aud_key(key, part):
    key = jax.random.fold_in(key, 14)
    return token_field(key, AUDIO, 1.5)


def draw_vid_lse(key, part):
    key = jax.random.fold_in(key, 21)
    offsets = jax.random.uniform(key, (HEADS, VIDEO), jnp.float32, 0.2, 1.0)
    return math.log(AUDIO) + offsets


def draw_aud_lse(key, part):
    key = jax.random.fold_in(key, 22)
    offsets = jax.random.uniform(key, (HEADS, AUDIO), jnp.float32, 0.2, 1.0)
    return math.log(VIDEO) + offsets


def place_ends(entries, key, smallest, top_value):
    place = [jax.random.randint(jax.random.fold_in(key, axis), (), 0, length) for axis, length in enumerate(entries.shape)]
    widest = entries.shape.index(max(entries.shape))
    neighbour = place[:widest] + [(place[widest] + 1) % entries.shape[widest]] + place[widest + 1:]
    return entries.at[tuple(place)].set(smallest).at[tuple(neighbour)].set(top_value)


def levels(stream_key, dims, cuts, low, largest):
    factor_of, own = 1.0, jax.random.fold_in(stream_key, 6)
    for dim, blocks in cuts:
        heights = jnp.exp(jax.random.uniform(jax.random.fold_in(own, dim), (blocks,), jnp.float32, low / len(cuts), largest / len(cuts)))
        factor_of = factor_of * jnp.repeat(heights, dims[dim] // blocks).reshape([-1 if axis == dim else 1 for axis in range(len(dims))])
    return factor_of


def centred(own_key, shape, spread, bound, cuts=(), kind=jnp.bfloat16):
    drawn = spread * jax.random.normal(own_key, shape, jnp.float32)
    if cuts:
        drawn = drawn * levels(own_key, shape, cuts, -0.22, 0.18)
    return jnp.clip(drawn, -bound, bound).astype(kind)


def setup_inputs(seed: int = 0) -> dict:
    keys = jax.random.split(jax.random.key(seed), 19)
    return {
        "vid_query": draw_vid_query(jax.random.fold_in(keys[18], 71), 0),
        "vid_key": draw_vid_key(jax.random.fold_in(keys[18], 71), 0),
        "vid_value": centred(keys[2], (HEADS, VIDEO, DH), 1.0, 6.0, ((0, 8), (1, 32))),
        "vid_out": centred(keys[3], (HEADS, VIDEO, DH), 1.0, 6.0, ((0, 8), (1, 32))),
        "vid_grad": centred(keys[4], (HEADS, VIDEO, DH), 16.0, 96.0, ((0, 8), (1, 32))),
        "vid_lse": draw_vid_lse(jax.random.fold_in(keys[18], 71), 0),
        "vid_mask": place_ends(jax.random.randint(keys[6], (HEADS, VIDEO, AUDIO // 8), 0, 256), jax.random.fold_in(keys[6], 1), 0, 255).astype(jnp.int32),
        "aud_query": draw_aud_query(jax.random.fold_in(keys[18], 71), 0),
        "aud_key": draw_aud_key(jax.random.fold_in(keys[18], 71), 0),
        "aud_value": centred(keys[9], (HEADS, AUDIO, DH), 1.0, 6.0, ((0, 8), (1, 32))),
        "aud_out": centred(keys[10], (HEADS, AUDIO, DH), 1.0, 6.0, ((0, 8), (1, 32))),
        "aud_grad": centred(keys[11], (HEADS, AUDIO, DH), 64.0, 384.0, ((0, 8), (1, 32))),
        "aud_lse": draw_aud_lse(jax.random.fold_in(keys[18], 71), 0),
        "aud_mask": place_ends(jax.random.randint(keys[13], (HEADS, AUDIO, VIDEO // 8), 0, 256), jax.random.fold_in(keys[13], 1), 0, 255).astype(jnp.int32),
        "gain_vq": jnp.clip(1.0 + 0.1 * jax.random.normal(keys[14], (HEADS, DH), jnp.float32), 0.5, 1.5),
        "gain_ak": jnp.clip(1.0 + 0.1 * jax.random.normal(keys[15], (HEADS, DH), jnp.float32), 0.5, 1.5),
        "gain_aq": jnp.clip(1.0 + 0.1 * jax.random.normal(keys[16], (HEADS, DH), jnp.float32), 0.5, 1.5),
        "gain_vk": jnp.clip(1.0 + 0.1 * jax.random.normal(keys[17], (HEADS, DH), jnp.float32), 0.5, 1.5),
    }


EPS = 1e-06

def unpack_bits(word_rows):
    shifts = jnp.arange(8, dtype=jnp.int32)
    bit_values = jnp.bitwise_and(jnp.right_shift(word_rows[..., None], shifts), 1)
    return bit_values.reshape(word_rows.shape[:-1] + (word_rows.shape[-1] * 8,)).astype(jnp.float32)

def row_scales(tokens):
    values = tokens.astype(jnp.float32)
    return lax.rsqrt(lax.optimization_barrier(jnp.mean(values * values, axis=(0, 2))) + EPS)

def normalize(tokens, scales, gain_rows):
    return (tokens.astype(jnp.float32) * scales[None, :, None] * gain_rows[:, None, :]).astype(jnp.bfloat16)

def norm_backward(tokens, scales, gain_rows, upstream):
    weighted = upstream * gain_rows[:, None, :]
    unit_rows = tokens.astype(jnp.float32) * scales[None, :, None]
    mean_term = lax.optimization_barrier(jnp.mean(weighted * unit_rows, axis=(0, 2)))
    return (scales[None, :, None] * (weighted - unit_rows * mean_term[None, :, None])).astype(jnp.bfloat16)

def one_direction(queries, key_rows, value_rows, outputs, upstream, lse_rows, word_rows):
    query_count, head_dim = queries.shape
    score_scale = head_dim ** (-0.5)
    block_rows = math.gcd(query_count, 512)
    block_count = query_count // block_rows
    stacked = (queries.reshape(block_count, block_rows, head_dim), upstream.reshape(block_count, block_rows, head_dim), outputs.reshape(block_count, block_rows, head_dim), lse_rows.reshape(block_count, block_rows), word_rows.reshape(block_count, block_rows, word_rows.shape[-1]))

    def sweep_block(running, pieces):
        key_grad, value_grad = running
        query_block, grad_block, out_block, lse_block, word_block = pieces
        scores = jnp.dot(query_block, key_rows.T, preferred_element_type=jnp.float32) * score_scale
        attention = jnp.exp(scores - lse_block[:, None])
        kept_mask = unpack_bits(word_block)
        dropped = (2.0 * kept_mask * attention).astype(jnp.bfloat16)
        value_grad = value_grad + jnp.dot(dropped.T, grad_block, preferred_element_type=jnp.float32)
        delta_rows = lax.optimization_barrier(jnp.sum(grad_block.astype(jnp.float32) * out_block.astype(jnp.float32), axis=1))
        prob_grad = 2.0 * kept_mask * jnp.dot(grad_block, value_rows.T, preferred_element_type=jnp.float32)
        score_grad = (attention * (prob_grad - delta_rows[:, None])).astype(jnp.bfloat16)
        query_grad = score_scale * jnp.dot(score_grad, key_rows, preferred_element_type=jnp.float32)
        key_grad = key_grad + score_scale * jnp.dot(score_grad.T, query_block, preferred_element_type=jnp.float32)
        return ((key_grad, value_grad), query_grad)
    empty_rows = jnp.zeros(key_rows.shape, jnp.float32)
    (key_grad, value_grad), query_grad = lax.scan(sweep_block, (empty_rows, empty_rows), stacked)
    return (query_grad.reshape(query_count, head_dim), key_grad, value_grad)

def reference(vid_query, vid_key, vid_value, vid_out, vid_grad, vid_lse, vid_mask, aud_query, aud_key, aud_value, aud_out, aud_grad, aud_lse, aud_mask, gain_vq, gain_ak, gain_aq, gain_vk):
    scale_vq = row_scales(vid_query)
    scale_ak = row_scales(aud_key)
    scale_aq = row_scales(aud_query)
    scale_vk = row_scales(vid_key)
    normed_vq = normalize(vid_query, scale_vq, gain_vq)
    normed_ak = normalize(aud_key, scale_ak, gain_ak)
    normed_aq = normalize(aud_query, scale_aq, gain_aq)
    normed_vk = normalize(vid_key, scale_vk, gain_vk)

    def per_head(head_items):
        video_q, audio_k, audio_v, video_o, video_g, video_l, video_w, audio_q, video_k, video_v, audio_o, audio_g, audio_l, audio_w = head_items
        up_vq, up_ak, grad_av = one_direction(video_q, audio_k, audio_v, video_o, video_g, video_l, video_w)
        up_aq, up_vk, grad_vv = one_direction(audio_q, video_k, video_v, audio_o, audio_g, audio_l, audio_w)
        return (up_vq, up_ak, grad_av, up_aq, up_vk, grad_vv)
    up_vq, up_ak, grad_av, up_aq, up_vk, grad_vv = lax.map(per_head, (normed_vq, normed_ak, aud_value, vid_out, vid_grad, vid_lse, vid_mask, normed_aq, normed_vk, vid_value, aud_out, aud_grad, aud_lse, aud_mask))
    grad_vid_query = norm_backward(vid_query, scale_vq, gain_vq, up_vq)
    grad_aud_key = norm_backward(aud_key, scale_ak, gain_ak, up_ak)
    grad_aud_query = norm_backward(aud_query, scale_aq, gain_aq, up_aq)
    grad_vid_key = norm_backward(vid_key, scale_vk, gain_vk, up_vk)
    return (grad_vid_query, grad_vid_key, grad_vv.astype(jnp.bfloat16), grad_aud_query, grad_aud_key, grad_av.astype(jnp.bfloat16))
```

```python
import functools
import math

import jax
import jax.numpy as jnp
from jax import lax
from jax.experimental import pallas as pl
from jax.experimental.pallas import tpu as pltpu
from jax.sharding import Mesh
from jax.sharding import PartitionSpec as P

EPS = 1e-06
LOG2E = math.log2(math.e)
F32 = jnp.float32
BF16 = jnp.bfloat16
PLANES, NEAR, CORES, HEAD_GROUPS = 8, 2, 2, 8
QUAD = NEAR * CORES
QUAD_AXES = ("near", "core")
CTX_AXES = ("plane", "near", "core")


def dot_nt(left, right):
    return lax.dot_general(left, right, (((1,), (1,)), ((), ())), preferred_element_type=F32)


def dot_nn(left, right):
    return lax.dot_general(left, right, (((1,), (0,)), ((), ())), preferred_element_type=F32)


def dot_tn(left, right):
    return lax.dot_general(left, right, (((0,), (0,)), ((), ())), preferred_element_type=F32)


def keep_rows(words):
    wide = words.astype(jnp.int32)
    return jnp.concatenate([jnp.bitwise_and(wide, 1 << bit) != 0 for bit in range(8)], axis=0)


def probs_and_scores(keys, values, queries, twice_grad, lse2, delta, kept, coefficient):
    probs = jnp.exp2(dot_nt(keys, queries) * coefficient - lse2)
    dropped = jnp.where(kept, probs, 0.0).astype(BF16)
    prob_grad = jnp.where(kept, dot_nt(values, twice_grad), 0.0)
    return dropped, (probs * (prob_grad - delta)).astype(BF16)


def attention_kernel(
    aud_k, aud_v, aud_q, aud_g, aud_l, aud_d, vid_k, vid_v, vid_q, vid_g, vid_l, vid_d,
    vid_words, aud_words, aud_out, vid_out, sum_k, sum_v, sum_q, *, scale
):
    step = pl.program_id(0)
    coefficient = scale * LOG2E

    @pl.when(step == 0)
    def _():
        sum_k[...] = jnp.zeros_like(sum_k)
        sum_v[...] = jnp.zeros_like(sum_v)
        sum_q[...] = jnp.zeros_like(sum_q)

    keys, values, queries, grads = aud_k[0], aud_v[0], aud_q[0], aud_g[0]
    kept = keep_rows(jnp.concatenate([vid_words[i] for i in range(vid_words.shape[0])], axis=1))
    dropped, score_grad = probs_and_scores(
        keys, values, vid_q[...], vid_g[...], vid_l[...], vid_d[...], kept, coefficient
    )
    aud_out[0, 0] = (dot_nn(score_grad, vid_q[...]) * scale).astype(aud_out.dtype)
    aud_out[0, 1] = dot_nn(dropped, vid_g[...]).astype(aud_out.dtype)
    sum_q[...] += dot_tn(score_grad, keys)
    kept = keep_rows(aud_words[...].reshape(-1, aud_words.shape[2]))
    dropped, score_grad = probs_and_scores(
        vid_k[...], vid_v[...], queries, grads, aud_l[0], aud_d[0], kept, coefficient
    )
    sum_v[...] += dot_nn(dropped, grads)
    sum_k[...] += dot_nn(score_grad, queries)
    aud_out[0, 2] = (dot_tn(score_grad, vid_k[...]) * scale).astype(aud_out.dtype)

    @pl.when(step == pl.num_programs(0) - 1)
    def _():
        vid_out[0] = (sum_k[...] * scale).astype(vid_out.dtype)
        vid_out[1] = sum_v[...].astype(vid_out.dtype)
        vid_out[2] = (sum_q[...] * scale).astype(vid_out.dtype)


def attention(aud, aud_rows, vid, vid_rows, vid_words, aud_words, scale):
    planes, rows, dim = aud[0].shape
    vid_count = vid[0].shape[0]
    whole = pl.BlockSpec((vid_count, dim), lambda c: (0, 0))
    line = pl.BlockSpec((1, vid_count), lambda c: (0, 0))
    block = pl.BlockSpec((1, rows, dim), lambda c: (c, 0, 0))
    block_line = pl.BlockSpec((1, 1, rows), lambda c: (c, 0, 0))
    pairs = 2 * planes * rows * vid_count
    return pl.pallas_call(
        functools.partial(attention_kernel, scale=scale),
        grid=(planes,),
        in_specs=[block] * 4 + [block_line] * 2 + [whole] * 4 + [line] * 2 + [
            pl.BlockSpec((vid_words.shape[0], rows // 8, vid_words.shape[2]), lambda c: (0, c, 0)),
            pl.BlockSpec((aud_words.shape[0], aud_words.shape[1], rows), lambda c: (0, 0, c)),
        ],
        out_specs=[
            pl.BlockSpec((1, 3, rows, dim), lambda c: (c, 0, 0, 0)),
            pl.BlockSpec((3, vid_count, dim), lambda c: (0, 0, 0)),
        ],
        out_shape=[
            jax.ShapeDtypeStruct((planes, 3, rows, dim), BF16),
            jax.ShapeDtypeStruct((3, vid_count, dim), BF16),
        ],
        scratch_shapes=[pltpu.VMEM((vid_count, dim), F32)] * 3,
        compiler_params=pltpu.CompilerParams(vmem_limit_bytes=56 * 2**20),
        cost_estimate=pl.CostEstimate(
            flops=10 * pairs * dim, bytes_accessed=8 * 2**20, transcendentals=pairs
        ),
    )(*aud, *aud_rows, *vid, *vid_rows, vid_words, aud_words)


def over_heads(sums):
    return jnp.sum(
        lax.all_to_all(
            jnp.broadcast_to(sums[None], (HEAD_GROUPS,) + sums.shape), "head", 0, 0, tiled=True
        ),
        axis=0,
    )


def square_sums(tokens):
    values = tokens.astype(F32)
    return jnp.sum(values * values, axis=(0, 2))


def bits_first(rows):
    split = rows.reshape(rows.shape[:-2] + (rows.shape[-2] // 8, 8, rows.shape[-1]))
    return jnp.swapaxes(split, -3, -2)


def to_quad(rows):
    return lax.all_to_all(rows, QUAD_AXES, 0, 0, tiled=True)


def normalize(tokens, scales, gain_row):
    return (tokens.astype(F32) * scales[..., None] * gain_row).astype(BF16)


def norm_parts(tokens, scales, gain_rows, upstream):
    weighted = upstream.astype(F32) * gain_rows[:, None, :]
    unit_rows = tokens.astype(F32) * scales[None, :, None]
    return weighted, unit_rows, jnp.sum(weighted * unit_rows, axis=(0, 2))


def norm_finish(weighted, unit_rows, scales, mean_term):
    return (scales[None, :, None] * (weighted - unit_rows * mean_term[None, :, None])).astype(BF16)


def local(
    vid_query, vid_key, vid_value, vid_out, vid_grad, vid_lse, vid_mask,
    aud_query, aud_key, aud_value, aud_out, aud_grad, aud_lse, aud_mask,
    gain_vq, gain_ak, gain_aq, gain_vk,
):
    heads, vid_rows, dim = vid_query.shape
    aud_rows = aud_query.shape[1]
    vid_words, aud_words = vid_rows // 8, aud_rows // 8
    plane_rows, quad_rows = QUAD * aud_rows, QUAD * vid_rows
    feature_count = HEAD_GROUPS * heads * dim
    scale = dim**-0.5

    audio = jnp.stack(
        [
            bits_first(aud_key).reshape(aud_key.shape),
            bits_first(aud_value).reshape(aud_value.shape),
            aud_query,
            aud_grad + aud_grad,
        ],
        axis=1,
    )
    audio = jnp.swapaxes(to_quad(audio), 0, 1)
    by_word = audio[:2].reshape(2, QUAD, 8, aud_words, dim).swapaxes(1, 2)
    audio = jnp.concatenate(
        [by_word.reshape(2, plane_rows, dim), audio[2:].reshape(2, plane_rows, dim)]
    )
    audio = lax.all_gather(audio, "plane", axis=0, tiled=False)

    sums = jnp.concatenate(
        [square_sums(vid_query), square_sums(vid_key), square_sums(aud_key), square_sums(aud_query)]
    )
    scales = lax.rsqrt(over_heads(sums) / feature_count + EPS)
    cuts = (vid_rows, 2 * vid_rows, 2 * vid_rows + aud_rows)
    scale_vq, scale_vk, scale_ak, scale_aq = jnp.split(scales, cuts)

    video = jnp.stack(
        [bits_first(vid_key).reshape(vid_key.shape), bits_first(vid_value).reshape(vid_key.shape),
         vid_query, vid_grad + vid_grad], axis=1,
    )
    video = jnp.swapaxes(to_quad(video), 0, 1)
    by_word = video[:2].reshape(2, QUAD, 8, vid_words, dim).swapaxes(1, 2)
    vid_k, vid_v = by_word.reshape(2, quad_rows, dim)
    vid_q, vid_g = video[2:].reshape(2, quad_rows, dim)
    words_v = to_quad(jnp.swapaxes(vid_mask.astype(jnp.int16), 1, 2))
    words_a = to_quad(jnp.swapaxes(aud_mask.astype(jnp.int16), 1, 2))

    delta_v = jnp.sum(vid_grad.astype(F32) * vid_out.astype(F32), axis=2)
    delta_a = jnp.sum(aud_grad.astype(F32) * aud_out.astype(F32), axis=2)

    def per_head(lse, delta, scale_a, scale_b):
        return jnp.stack(
            [lse * LOG2E, delta, jnp.broadcast_to(scale_a, lse.shape), jnp.broadcast_to(scale_b, lse.shape)],
            axis=1,
        )

    small_a = per_head(aud_lse, delta_a, scale_ak, scale_aq)
    small_a = lax.all_to_all(
        jnp.broadcast_to(small_a[None], (PLANES,) + small_a.shape).reshape(PLANES * QUAD, 4, aud_rows),
        CTX_AXES, 0, 0, tiled=True,
    )
    small_a = small_a.reshape(PLANES, QUAD, 4, aud_rows).swapaxes(1, 2)
    lse_a, sums_a, whole_ak, whole_aq = jnp.moveaxis(small_a, 1, 0)
    whole_ak = whole_ak.reshape(PLANES, QUAD, aud_words, 8).transpose(0, 3, 1, 2).reshape(PLANES, plane_rows)
    whole_aq = whole_aq.reshape(PLANES, plane_rows)
    small_v = jnp.swapaxes(to_quad(per_head(vid_lse, delta_v, scale_vk, scale_vq)), 0, 1)
    lse_v, sums_v, whole_vk, whole_vq = small_v
    whole_vk = whole_vk.reshape(QUAD, vid_words, 8).transpose(2, 0, 1).reshape(quad_rows)
    whole_vq = whole_vq.reshape(quad_rows)

    own = lax.axis_index(QUAD_AXES)

    def own_gain(gain):
        return lax.dynamic_index_in_dim(gain, own, 0, keepdims=False)

    aud_sets = (
        normalize(audio[:, 0], whole_ak, own_gain(gain_ak)),
        audio[:, 1],
        normalize(audio[:, 2], whole_aq, own_gain(gain_aq)),
        audio[:, 3],
    )
    vid_sets = (
        normalize(vid_k, whole_vk, own_gain(gain_vk)),
        vid_v,
        normalize(vid_q, whole_vq, own_gain(gain_vq)),
        vid_g,
    )
    aud_parts, vid_parts = attention(
        aud_sets,
        (lse_a.reshape(PLANES, 1, plane_rows), sums_a.reshape(PLANES, 1, plane_rows)),
        vid_sets,
        (lse_v.reshape(1, quad_rows), sums_v.reshape(1, quad_rows)),
        words_v, words_a, scale,
    )
    aud_total = lax.psum_scatter(aud_parts, "plane", scatter_dimension=0, tiled=True)[0]

    def back(parts, words):
        by_bit = parts[:2].reshape(2, 8, QUAD, words, dim).transpose(2, 0, 3, 1, 4)
        by_row = parts[2].reshape(QUAD, 1, 8 * words, dim)
        home = jnp.concatenate([by_bit.reshape(QUAD, 2, 8 * words, dim), by_row], axis=1)
        return jnp.swapaxes(to_quad(home), 0, 1)

    up_vk, grad_vv, up_vq = back(vid_parts, vid_words)
    weighted_vq, unit_vq, local_vq = norm_parts(vid_query, scale_vq, gain_vq, up_vq)
    weighted_vk, unit_vk, local_vk = norm_parts(vid_key, scale_vk, gain_vk, up_vk)
    mean_vq, mean_vk = over_heads(jnp.stack([local_vq, local_vk])) / feature_count
    grad_vid_query = norm_finish(weighted_vq, unit_vq, scale_vq, mean_vq)
    grad_vid_key = norm_finish(weighted_vk, unit_vk, scale_vk, mean_vk)

    up_ak, grad_av, up_aq = back(aud_total, aud_words)
    weighted_ak, unit_ak, local_ak = norm_parts(aud_key, scale_ak, gain_ak, up_ak)
    weighted_aq, unit_aq, local_aq = norm_parts(aud_query, scale_aq, gain_aq, up_aq)
    mean_ak, mean_aq = over_heads(jnp.stack([local_ak, local_aq])) / feature_count
    grad_aud_key = norm_finish(weighted_ak, unit_ak, scale_ak, mean_ak)
    grad_aud_query = norm_finish(weighted_aq, unit_aq, scale_aq, mean_aq)
    return grad_vid_query, grad_vid_key, grad_vv, grad_aud_query, grad_aud_key, grad_av


def solution(mesh):
    fine = Mesh(
        mesh.devices.reshape(PLANES, NEAR, CORES, HEAD_GROUPS), ("plane", "near", "core", "head")
    )
    rows, lines, gain = P("head", CTX_AXES, None), P("head", CTX_AXES), P("head", None)
    return jax.shard_map(
        local,
        mesh=fine,
        in_specs=(rows,) * 5 + (lines, rows) + (rows,) * 5 + (lines, P("head", None, CTX_AXES)) + (gain,) * 4,
        out_specs=(rows,) * 6,
        check_vma=False,
    )
```

```python
import functools
import math

import jax
import jax.numpy as jnp
from jax import lax
from jax.experimental import pallas as pl
from jax.experimental.pallas import tpu as pltpu
from jax.sharding import Mesh
from jax.sharding import PartitionSpec as P

EPS = 1e-06
LOG2E = math.log2(math.e)
F32 = jnp.float32
BF16 = jnp.bfloat16
PLANES, NEAR, CORES, HEAD_GROUPS = 8, 2, 2, 8
QUAD = NEAR * CORES
LINES = 16
QUAD_AXES = ("near", "core")
CTX_AXES = ("plane", "near", "core")


def dot_nt(left, right):
    return lax.dot_general(left, right, (((1,), (1,)), ((), ())), preferred_element_type=F32)


def dot_nn(left, right):
    return lax.dot_general(left, right, (((1,), (0,)), ((), ())), preferred_element_type=F32)


def dot_tn(left, right):
    return lax.dot_general(left, right, (((0,), (0,)), ((), ())), preferred_element_type=F32)


def keep_rows(words, group):
    wide = words.astype(F32).astype(jnp.int32)
    picked = [
        jnp.bitwise_and(wide[first : first + group], 1 << bit)
        for first in range(0, words.shape[0], group)
        for bit in range(8)
    ]
    return jnp.concatenate(picked, axis=0) != 0


def probs_and_scores(keys, values, queries, twice_grad, lse2, delta, kept, coefficient):
    probs = jnp.exp2(dot_nt(keys, queries) * coefficient - lse2)
    dropped = jnp.where(kept, probs, 0.0).astype(BF16)
    prob_grad = jnp.where(kept, dot_nt(values, twice_grad), 0.0)
    return dropped, (probs * (prob_grad - delta)).astype(BF16)


def attention_kernel(ids, *refs, scale, count, first, last):
    coefficient = scale * LOG2E
    pieces = QUAD
    refs = list(refs)

    def take(number):
        taken, refs[:number] = refs[:number], []
        return taken

    per_plane = [(take(1)[0], take(1)[0], take(pieces), take(pieces)) for _ in range(count)]
    vid_kv, vid_qg, vid_small = take(pieces), take(pieces), take(pieces)
    if not first:
        sums_in, refs = refs[0], refs[1:]
    aud_out, vid_out = refs[:2]
    own = ids[0]
    rows, wide = vid_kv[0].shape
    dim = wide // 2

    def joined(blocks, axis=0):
        return jnp.concatenate([block[...] for block in blocks], axis=axis)

    both = joined(vid_kv)
    k_v, v_v = both[:, :dim], both[:, dim:]
    both = joined(vid_qg)
    q_v, g_v = both[:, :dim], both[:, dim:]
    small = joined(vid_small, 1).astype(F32)
    small = small[0:2] + small[2:4] + small[4:6]
    lse_v, delta_v = small[0:1], small[1:2]
    sums = [jnp.zeros((pieces * rows, dim), F32) if first else sums_in[i] for i in range(3)]
    for i, (aud_kv, aud_qg, words_v, words_a) in enumerate(per_plane):
        k_a, v_a = aud_kv[:rows], aud_kv[rows : 2 * rows]
        q_a, g_a = aud_qg[:rows], aud_qg[rows : 2 * rows]
        small = aud_qg[2 * rows :].astype(F32)
        small = small[0:4] + small[4:8] + small[8:12]
        lse_a, delta_a = [
            jnp.concatenate([small[j : j + 1], small[j + 1 : j + 2]], axis=1) for j in (0, 2)
        ]
        kept = keep_rows(joined(words_v, 1), 8)
        dropped, score_grad = probs_and_scores(
            k_a, v_a, q_v, g_v, lse_v, delta_v, kept, coefficient
        )
        aud_out[i, 0] = dot_nn(score_grad, q_v) * scale
        aud_out[i, 1] = dot_nn(dropped, g_v)
        sums[2] = sums[2] + dot_tn(score_grad, k_a)
        kept = keep_rows(joined(words_a), rows // 8)
        dropped, score_grad = probs_and_scores(
            k_v, v_v, q_a, g_a, lse_a, delta_a, kept, coefficient
        )
        sums[1] = sums[1] + dot_nn(dropped, g_a)
        sums[0] = sums[0] + dot_nn(score_grad, q_a)
        aud_out[i, 2] = dot_tn(score_grad, k_v) * scale
    if last:
        sums = [sums[0] * scale, sums[1], sums[2] * scale]
        for i in range(pieces):
            for j in range(3):
                vid_out[jnp.bitwise_xor(own, i), j] = sums[j][i * rows : (i + 1) * rows].astype(BF16)
    else:
        for j in range(3):
            vid_out[j] = sums[j]


def attention(ids, planes, words, video, sums, last, scale):
    count, first = len(planes), sums is None
    pieces, wide = len(video), video[0].shape[1]
    dim, rows = wide // 2, wide
    plane_words, vid_count = rows // 8, pieces * rows
    specs, operands = [], []

    def add(array, shape, index):
        operands.append(array)
        specs.append(pl.BlockSpec(shape, index))

    for i, halves in enumerate(planes):
        if len(halves) == 1:
            add(halves[0], (2 * rows, dim), lambda c, s: (0, 0))
            add(halves[0], (pl.Element(2 * rows + LINES), pl.Element(dim)), lambda c, s: (2 * rows, 0))
        else:
            for half in halves:
                add(half, half.shape, lambda c, s: (0, 0))
        for piece in video:
            add(piece, (plane_words, wide), lambda c, s, i=i: (2 * rows // plane_words + s[1 + i], 0))
        for piece in words:
            add(piece, (plane_words, wide), lambda c, s, i=i: (s[1 + i], 0))
    for depth, place in ((rows, 0), (rows, 1), (LINES, 3 * rows // LINES)):
        for piece in video:
            add(piece, (depth, wide), lambda c, s, place=place: (place, 0))
    if not first:
        add(sums, sums.shape, lambda c, s: (0, 0, 0))
    if last:
        vid_shape, vid_type = (pieces, 3, rows, dim), BF16
    else:
        vid_shape, vid_type = (3, vid_count, dim), F32
    pairs = 2 * count * rows * vid_count
    return pl.pallas_call(
        functools.partial(attention_kernel, scale=scale, count=count, first=first, last=last),
        grid_spec=pltpu.PrefetchScalarGridSpec(
            num_scalar_prefetch=1,
            grid=(1,),
            in_specs=specs,
            out_specs=[
                pl.BlockSpec((count, 3, rows, dim), lambda c, s: (0, 0, 0, 0)),
                pl.BlockSpec(vid_shape, lambda c, s: (0,) * len(vid_shape)),
            ],
        ),
        out_shape=[
            jax.ShapeDtypeStruct((count, 3, rows, dim), F32),
            jax.ShapeDtypeStruct(vid_shape, vid_type),
        ],
        compiler_params=pltpu.CompilerParams(vmem_limit_bytes=32 * 2**20),
        cost_estimate=pl.CostEstimate(
            flops=10 * pairs * dim, bytes_accessed=4 * 2**20, transcendentals=pairs
        ),
    )(ids, *operands)


def from_heads(lines):
    return lax.all_to_all(lines, "head", 0, 0, tiled=True)


def row_line(values):
    return jnp.sum(values.T, axis=0, keepdims=True)


def columns(line, dim):
    return jnp.broadcast_to(line, (dim, line.shape[1])).T


def sums_kernel(aud_k, aud_q, vid_q, vid_k, out):
    lines = []
    pair = []
    for tokens in (aud_k, aud_q, vid_q, vid_k):
        total = 0.0
        for i in range(tokens.shape[0]):
            values = tokens[i].astype(F32)
            total = total + values * values
        pair.append(total)
    both = jnp.concatenate(pair[:2], axis=0)
    line = jnp.concatenate([row_line(both), row_line(pair[2]), row_line(pair[3])], axis=1)
    out[...] = jnp.broadcast_to(line, out.shape)


def head_sums(aud_k, aud_q, vid_q, vid_k):
    rows = 2 * (aud_k.shape[1] + vid_k.shape[1])
    return pl.pallas_call(
        sums_kernel,
        out_shape=jax.ShapeDtypeStruct((HEAD_GROUPS, rows), F32),
        compiler_params=pltpu.CompilerParams(vmem_limit_bytes=16 * 2**20),
    )(aud_k, aud_q, vid_q, vid_k)


def bit_order(values):
    words = values.shape[0] // 8
    return jnp.swapaxes(values.reshape(words, 8, values.shape[1]), 0, 1).reshape(values.shape)


def word_order(values):
    words = values.shape[0] // 8
    return jnp.swapaxes(values.reshape(8, words, values.shape[1]), 0, 1).reshape(values.shape)


def pack_kernel(sums, aud_k, aud_v, aud_q, aud_g, lines, gain_k, gain_q, out, scales, *, features):
    total = jnp.sum(sums[...], axis=0, keepdims=True)
    line = lax.rsqrt(total / features + EPS)
    scales[...] = line
    heads, rows, dim = aud_k.shape
    column = columns(line[:, : 2 * rows], dim)
    for i in range(heads):
        k = (aud_k[i].astype(F32) * column[:rows] * gain_k[i : i + 1]).astype(BF16)
        out[i, :rows] = bit_order(k.astype(F32)).astype(BF16)
        out[i, rows : 2 * rows] = bit_order(aud_v[i].astype(F32)).astype(BF16)
        out[i, 2 * rows : 3 * rows] = (
            aud_q[i].astype(F32) * column[rows:] * gain_q[i : i + 1]
        ).astype(BF16)
        out[i, 3 * rows : 4 * rows] = (2.0 * aud_g[i].astype(F32)).astype(BF16)
        out[i, 4 * rows :] = lines[i]


def pack_audio(sums, aud_k, aud_v, aud_q, aud_g, lines, gain_k, gain_q, features):
    heads, rows, dim = aud_k.shape
    return pl.pallas_call(
        functools.partial(pack_kernel, features=features),
        out_shape=[
            jax.ShapeDtypeStruct((heads, 4 * rows + LINES, dim), BF16),
            jax.ShapeDtypeStruct((1, sums.shape[1]), F32),
        ],
        compiler_params=pltpu.CompilerParams(vmem_limit_bytes=16 * 2**20),
    )(sums, aud_k, aud_v, aud_q, aud_g, lines, gain_k, gain_q)


def finish_kernel(means, scales, *refs, features):
    (aud_k, aud_q, vid_q, vid_k, up_ak, up_aq, up_vq, up_vk,
     gain_ak, gain_aq, gain_vq, gain_vk, out_ak, out_aq, out_vq, out_vk) = refs
    mean_line = jnp.sum(means[...], axis=0, keepdims=True) / features
    scale_line = scales[...]
    heads, rows, dim = aud_k.shape
    cut = 2 * rows
    more = vid_q.shape[1]
    places = [(0, rows, True), (rows, cut, False), (cut, cut + more, False), (cut + more, cut + 2 * more, True)]
    scale_col = columns(scale_line, dim)
    mean_col = columns(mean_line, dim)
    sets = (
        (aud_k, up_ak, gain_ak, out_ak), (aud_q, up_aq, gain_aq, out_aq),
        (vid_q, up_vq, gain_vq, out_vq), (vid_k, up_vk, gain_vk, out_vk),
    )
    for (tokens, up, gain, out), (first, last, bits) in zip(sets, places):
        scale, mean = scale_col[first:last], mean_col[first:last]
        for i in range(heads):
            upstream = up[i].astype(F32)
            if bits:
                upstream = word_order(upstream)
            weighted = upstream * gain[i : i + 1]
            unit = tokens[i].astype(F32) * scale
            out[i] = (scale * (weighted - unit * mean)).astype(BF16)


def finish(means, scales, tokens, ups, gains, features):
    return pl.pallas_call(
        functools.partial(finish_kernel, features=features),
        out_shape=[jax.ShapeDtypeStruct(t.shape, BF16) for t in tokens],
        compiler_params=pltpu.CompilerParams(vmem_limit_bytes=32 * 2**20),
    )(means, scales, *tokens, *ups, *gains)
def pack_video_kernel(
    own, scales, vid_k, vid_v, vid_q, vid_g, mask, lines, gain_k, gain_q, *outs
):
    heads, rows, dim = vid_k.shape
    first = scales.shape[1] - 2 * rows
    column_q = columns(scales[:, first : first + rows], dim)
    column_k = columns(scales[:, first + rows :], dim)
    for i, out in enumerate(outs):
        head = jnp.bitwise_xor(own[0], i)
        k = (vid_k[head].astype(F32) * column_k * gain_k[pl.ds(head, 1), :]).astype(BF16)
        out[:rows, :dim] = bit_order(k.astype(F32)).astype(BF16)
        out[:rows, dim:] = bit_order(vid_v[head].astype(F32)).astype(BF16)
        out[rows : 2 * rows, :dim] = (
            vid_q[head].astype(F32) * column_q * gain_q[pl.ds(head, 1), :]
        ).astype(BF16)
        out[rows : 2 * rows, dim:] = (2.0 * vid_g[head].astype(F32)).astype(BF16)
        out[2 * rows : 3 * rows] = mask[head].astype(F32).T.astype(BF16)
        out[3 * rows :] = lines[head]


def pack_video(own, scales, vid_k, vid_v, vid_q, vid_g, mask, lines, gain_k, gain_q):
    heads, rows, dim = vid_k.shape
    smem = pl.BlockSpec(memory_space=pltpu.SMEM)
    vmem = pl.BlockSpec(memory_space=pltpu.VMEM)
    return pl.pallas_call(
        pack_video_kernel,
        in_specs=[smem] + [vmem] * 9,
        out_shape=[jax.ShapeDtypeStruct((3 * rows + LINES, 2 * dim), BF16)] * heads,
        compiler_params=pltpu.CompilerParams(vmem_limit_bytes=16 * 2**20),
    )(own, scales, vid_k, vid_v, vid_q, vid_g, mask, lines, gain_k, gain_q)


def pack_words_kernel(own, mask, *outs):
    for i, out in enumerate(outs):
        words = mask[jnp.bitwise_xor(own[0], i)].astype(F32).astype(BF16)
        count, wide = words.shape[0], out.shape[1]
        for j in range(words.shape[1] // wide):
            out[j * count : (j + 1) * count] = words[:, j * wide : (j + 1) * wide]


def pack_words(own, mask, wide):
    heads, count, queries = mask.shape
    return pl.pallas_call(
        pack_words_kernel,
        in_specs=[pl.BlockSpec(memory_space=pltpu.SMEM), pl.BlockSpec(memory_space=pltpu.VMEM)],
        out_shape=[jax.ShapeDtypeStruct((count * queries // wide, wide), BF16)] * heads,
        compiler_params=pltpu.CompilerParams(vmem_limit_bytes=16 * 2**20),
    )(own, mask)


def words_first(rows):
    split = rows.reshape(rows.shape[:-2] + (8, rows.shape[-2] // 8, rows.shape[-1]))
    return jnp.swapaxes(split, -3, -2).reshape(rows.shape)


def to_quad(rows):
    return lax.all_to_all(rows, QUAD_AXES, 0, 0, tiled=True)


def shift(rows, step):
    return lax.ppermute(rows, "plane", [(i, (i + step) % PLANES) for i in range(PLANES)])


def after(value, *others):
    return lax.optimization_barrier((value,) + others)[0]


def token_sums(tokens, scales, gain_rows, upstream):
    weighted = upstream.astype(F32) * gain_rows[:, None, :]
    return jnp.sum(weighted * (tokens.astype(F32) * scales[None, :, None]), axis=(0, 2))


def local(
    vid_query, vid_key, vid_value, vid_out, vid_grad, vid_lse, vid_mask,
    aud_query, aud_key, aud_value, aud_out, aud_grad, aud_lse, aud_mask,
    gain_vq, gain_ak, gain_aq, gain_vk,
):
    heads, vid_rows, dim = vid_query.shape
    aud_rows = aud_query.shape[1]
    plane_rows = QUAD * aud_rows
    feature_count = HEAD_GROUPS * heads * dim
    scale = dim**-0.5
    own_plane = lax.axis_index("plane")
    own = lax.axis_index(QUAD_AXES)

    own_line = own.astype(jnp.int32).reshape(1)

    sums = head_sums(aud_key, aud_query, vid_query, vid_key)
    arrived = from_heads(sums)

    def lines(lse, out, grad):
        delta = jnp.sum(grad.astype(F32) * out.astype(F32), axis=2)
        rest, found = jnp.stack([lse * LOG2E, delta], axis=1), []
        for _ in range(3):
            found.append(lax.reduce_precision(rest, 8, 7))
            rest = rest - found[-1]
        return jnp.stack(found, axis=1).astype(BF16)

    aud_lines = jnp.pad(
        lines(aud_lse, aud_out, aud_grad).reshape(heads, -1, dim),
        ((0, 0), (0, LINES - 6 * aud_rows // dim), (0, 0)),
    )
    vid_lines = jnp.pad(
        lines(vid_lse, vid_out, vid_grad).reshape(heads, 6, vid_rows),
        ((0, 0), (0, LINES - 6), (0, 0)),
    )

    def across_quad(pieces):
        return [pieces[0]] + [
            lax.ppermute(pieces[offset], QUAD_AXES, [(i, i ^ offset) for i in range(QUAD)])
            for offset in range(1, QUAD)
        ]

    words = across_quad(pack_words(after(own_line, sums), jnp.swapaxes(aud_mask, 1, 2), plane_rows))

    audio, scales = pack_audio(
        arrived, aud_key, aud_value, aud_query, aud_grad, aud_lines, gain_ak, gain_aq, feature_count
    )
    video = across_quad(
        pack_video(
            after(own_line, audio), scales, vid_key, vid_value, vid_query, vid_grad, vid_mask,
            vid_lines, gain_vk, gain_vq,
        )
    )
    audio = to_quad(audio)
    mine = audio[:, : 4 * aud_rows].reshape(QUAD, 4, aud_rows, dim).swapaxes(0, 1)
    tail = audio[:, 4 * aud_rows : 4 * aud_rows + 6 * aud_rows // dim].reshape(QUAD, 6, aud_rows)
    tail = tail.swapaxes(0, 1).reshape(6 * plane_rows // dim, dim)
    mine = jnp.concatenate(
        [mine.reshape(4 * plane_rows, dim), jnp.pad(tail, ((0, LINES - tail.shape[0]), (0, 0)))]
    )
    below, above = [mine], [mine]
    for _ in range(3):
        below.append(shift(below[-1], 1))
        above.append(shift(above[-1], -1))
    half = 2 * plane_rows
    far_kv, far_qg = shift(below[-1][:half], 1), shift(above[-1][half:], -1)

    def plane_ids(*offsets):
        return jnp.stack([own.astype(jnp.int32)] + [(own_plane + o) % PLANES for o in offsets]).astype(jnp.int32)

    part_near, total = attention(
        plane_ids(0, -1, 1), [(mine,), (below[1],), (above[1],)], words, video, None, False, scale
    )
    part_2, total = attention(
        plane_ids(-2, 2), [(below[2],), (above[2],)], words, video, total, False, scale
    )
    part_3, total = attention(
        plane_ids(-3, 3), [(below[3],), (above[3],)], words, video, total, False, scale
    )
    down = shift(part_3[0].astype(BF16), -1)
    part_far, vid_parts = attention(
        plane_ids(4), [(far_kv, far_qg)], words, video, total, True, scale
    )
    up = shift(part_far[0].astype(BF16), 1)

    def onward(part, arrived, step):
        return shift((part + arrived.astype(F32)).astype(BF16), step)

    up = onward(part_3[1], up, 1)
    up, down = onward(part_2[1], up, 1), onward(part_2[0], down, -1)
    up, down = onward(part_near[2], up, 1), onward(part_near[1], down, -1)
    aud_parts = (part_near[0] + up.astype(F32) + down.astype(F32)).astype(BF16)

    cuts = (aud_rows, 2 * aud_rows, 2 * aud_rows + vid_rows)
    scale_ak, scale_aq, scale_vq, scale_vk = jnp.split(scales[0], cuts)
    up_vk, grad_vv, up_vq = jnp.swapaxes(to_quad(vid_parts), 0, 1)
    grad_vv = words_first(grad_vv)
    local_vq = token_sums(vid_query, scale_vq, gain_vq, up_vq)
    local_vk = token_sums(vid_key, scale_vk, gain_vk, words_first(up_vk))

    home = aud_parts.reshape(3, QUAD, aud_rows, dim).swapaxes(0, 1)
    up_ak, grad_av, up_aq = jnp.swapaxes(to_quad(home), 0, 1)
    grad_av = words_first(grad_av)
    local_ak = token_sums(aud_key, scale_ak, gain_ak, words_first(up_ak))
    local_aq = token_sums(aud_query, scale_aq, gain_aq, up_aq)

    means = jnp.concatenate([local_ak, local_aq, local_vq, local_vk])
    means = from_heads(jnp.broadcast_to(means[None], (HEAD_GROUPS,) + means.shape))
    grad_ak, grad_aq, grad_vq, grad_vk = finish(
        means, scales, (aud_key, aud_query, vid_query, vid_key), (up_ak, up_aq, up_vq, up_vk),
        (gain_ak, gain_aq, gain_vq, gain_vk), feature_count,
    )
    return grad_vq, grad_vk, grad_vv, grad_aq, grad_ak, grad_av


def solution(mesh):
    fine = Mesh(
        mesh.devices.reshape(PLANES, NEAR, CORES, HEAD_GROUPS), ("plane", "near", "core", "head")
    )
    rows, lines, gain = P("head", CTX_AXES, None), P("head", CTX_AXES), P("head", None)
    return jax.shard_map(
        local,
        mesh=fine,
        in_specs=(rows,) * 5 + (lines, rows) + (rows,) * 5 + (lines, P("head", None, CTX_AXES)) + (gain,) * 4,
        out_specs=(rows,) * 6,
        check_vma=False,
    )
```

```python
import functools
import math

import jax
import jax.numpy as jnp
from jax import lax
from jax.experimental import pallas as pl
from jax.experimental.pallas import tpu as pltpu
from jax.sharding import Mesh
from jax.sharding import PartitionSpec as P

EPS = 1e-06
LOG2E = math.log2(math.e)
F32 = jnp.float32
BF16 = jnp.bfloat16
PLANES, NEAR, CORES, HEAD_GROUPS = 8, 2, 2, 8
QUAD = NEAR * CORES
LINES = 16
QUAD_AXES = ("near", "core")
CTX_AXES = ("plane", "near", "core")


def dot_nt(left, right):
    return lax.dot_general(left, right, (((1,), (1,)), ((), ())), preferred_element_type=F32)


def dot_nn(left, right):
    return lax.dot_general(left, right, (((1,), (0,)), ((), ())), preferred_element_type=F32)


def dot_tn(left, right):
    return lax.dot_general(left, right, (((0,), (0,)), ((), ())), preferred_element_type=F32)


def keep_rows(words, group):
    wide = words.astype(F32).astype(jnp.int32)
    picked = [
        jnp.bitwise_and(wide[first : first + group], 1 << bit)
        for first in range(0, words.shape[0], group)
        for bit in range(8)
    ]
    return jnp.concatenate(picked, axis=0) != 0


def probs_and_scores(keys, values, queries, twice_grad, lse2, delta, kept, coefficient):
    probs = jnp.exp2(dot_nt(keys, queries) * coefficient - lse2)
    dropped = jnp.where(kept, probs, 0.0).astype(BF16)
    prob_grad = jnp.where(kept, dot_nt(values, twice_grad), 0.0)
    return dropped, (probs * (prob_grad - delta)).astype(BF16)


def attention_kernel(ids, *refs, scale, count, first, last):
    coefficient = scale * LOG2E
    pieces = QUAD
    refs = list(refs)

    def take(number):
        taken, refs[:number] = refs[:number], []
        return taken

    per_plane = [(take(1)[0], take(1)[0], take(pieces), take(pieces)) for _ in range(count)]
    vid_kv, vid_qg, vid_small = take(pieces), take(pieces), take(pieces)
    if not first:
        sums_in, refs = refs[0], refs[1:]
    aud_out, vid_out = refs[:2]
    own = ids[0]
    rows, wide = vid_kv[0].shape
    dim = wide // 2

    def joined(blocks, axis=0):
        return jnp.concatenate([block[...] for block in blocks], axis=axis)

    both = joined(vid_kv)
    k_v, v_v = both[:, :dim], both[:, dim:]
    both = joined(vid_qg)
    q_v, g_v = both[:, :dim], both[:, dim:]
    small = joined(vid_small, 1).astype(F32)
    small = small[0:2] + small[2:4] + small[4:6]
    lse_v, delta_v = small[0:1], small[1:2]
    sums = [jnp.zeros((pieces * rows, dim), F32) if first else sums_in[i] for i in range(3)]
    for i, (aud_kv, aud_qg, words_v, words_a) in enumerate(per_plane):
        k_a, v_a = aud_kv[:rows], aud_kv[rows : 2 * rows]
        q_a, g_a = aud_qg[:rows], aud_qg[rows : 2 * rows]
        small = aud_qg[2 * rows :].astype(F32)
        small = [small[j : j + 1] + small[j + 1 : j + 2] + small[j + 2 : j + 3] for j in range(0, 12, 3)]
        turned = [pltpu.roll(values, dim // 2, 1) for values in small]
        left = lax.broadcasted_iota(jnp.int32, (1, dim), 1) < dim // 2
        lse_a = [jnp.where(left, small[j], turned[j + 1]) for j in (0, 2)]
        delta_a = [jnp.where(left, turned[j], small[j + 1]) for j in (0, 2)]
        lse_a, delta_a = jnp.concatenate(lse_a, axis=1), jnp.concatenate(delta_a, axis=1)
        kept = keep_rows(joined(words_v, 1), 8)
        dropped, score_grad = probs_and_scores(
            k_a, v_a, q_v, g_v, lse_v, delta_v, kept, coefficient
        )
        aud_out[i, 0] = dot_nn(score_grad, q_v) * scale
        aud_out[i, 1] = dot_nn(dropped, g_v)
        sums[2] = sums[2] + dot_tn(score_grad, k_a)
        kept = keep_rows(joined(words_a), rows // 8)
        dropped, score_grad = probs_and_scores(
            k_v, v_v, q_a, g_a, lse_a, delta_a, kept, coefficient
        )
        sums[1] = sums[1] + dot_nn(dropped, g_a)
        sums[0] = sums[0] + dot_nn(score_grad, q_a)
        aud_out[i, 2] = dot_tn(score_grad, k_v) * scale
    if last:
        sums = [sums[0] * scale, sums[1], sums[2] * scale]
        for i in range(pieces):
            for j in range(3):
                vid_out[jnp.bitwise_xor(own, i), j] = sums[j][i * rows : (i + 1) * rows].astype(BF16)
    else:
        for j in range(3):
            vid_out[j] = sums[j]


def attention(ids, planes, words, video, sums, last, scale):
    count, first = len(planes), sums is None
    pieces, wide = len(video), video[0].shape[1]
    dim, rows = wide // 2, wide
    plane_words, vid_count = rows // 8, pieces * rows
    specs, operands = [], []

    def add(array, shape, index):
        operands.append(array)
        specs.append(pl.BlockSpec(shape, index))

    for i, halves in enumerate(planes):
        if len(halves) == 1:
            add(halves[0], (2 * rows, dim), lambda c, s: (0, 0))
            add(halves[0], (pl.Element(2 * rows + LINES), pl.Element(dim)), lambda c, s: (2 * rows, 0))
        else:
            for half in halves:
                add(half, half.shape, lambda c, s: (0, 0))
        for piece in video:
            add(piece, (plane_words, wide), lambda c, s, i=i: (2 * rows // plane_words + s[1 + i], 0))
        for piece in words:
            add(piece, (plane_words, wide), lambda c, s, i=i: (s[1 + i], 0))
    for depth, place in ((rows, 0), (rows, 1), (LINES, 3 * rows // LINES)):
        for piece in video:
            add(piece, (depth, wide), lambda c, s, place=place: (place, 0))
    if not first:
        add(sums, sums.shape, lambda c, s: (0, 0, 0))
    if last:
        vid_shape, vid_type = (pieces, 3, rows, dim), BF16
    else:
        vid_shape, vid_type = (3, vid_count, dim), F32
    pairs = 2 * count * rows * vid_count
    return pl.pallas_call(
        functools.partial(attention_kernel, scale=scale, count=count, first=first, last=last),
        grid_spec=pltpu.PrefetchScalarGridSpec(
            num_scalar_prefetch=1,
            grid=(1,),
            in_specs=specs,
            out_specs=[
                pl.BlockSpec((count, 3, rows, dim), lambda c, s: (0, 0, 0, 0)),
                pl.BlockSpec(vid_shape, lambda c, s: (0,) * len(vid_shape)),
            ],
        ),
        out_shape=[
            jax.ShapeDtypeStruct((count, 3, rows, dim), F32),
            jax.ShapeDtypeStruct(vid_shape, vid_type),
        ],
        compiler_params=pltpu.CompilerParams(vmem_limit_bytes=32 * 2**20),
        cost_estimate=pl.CostEstimate(
            flops=10 * pairs * dim, bytes_accessed=4 * 2**20, transcendentals=pairs
        ),
    )(ids, *operands)


def from_heads(lines):
    return lax.all_to_all(lines, "head", 0, 0, tiled=True)


def row_line(values):
    return jnp.sum(values.T, axis=0, keepdims=True)


def columns(line, dim):
    return jnp.broadcast_to(line, (dim, line.shape[1])).T


def sums_kernel(aud_k, aud_q, vid_q, vid_k, out):
    lines = []
    pair = []
    for tokens in (aud_k, aud_q, vid_q, vid_k):
        total = 0.0
        for i in range(tokens.shape[0]):
            values = tokens[i].astype(F32)
            total = total + values * values
        pair.append(total)
    both = jnp.concatenate(pair[:2], axis=0)
    line = jnp.concatenate([row_line(both), row_line(pair[2]), row_line(pair[3])], axis=1)
    for i in range(out.shape[0]):
        out[i] = line


def head_sums(aud_k, aud_q, vid_q, vid_k):
    rows = 2 * (aud_k.shape[1] + vid_k.shape[1])
    return pl.pallas_call(
        sums_kernel,
        out_shape=jax.ShapeDtypeStruct((HEAD_GROUPS, 1, rows), F32),
        compiler_params=pltpu.CompilerParams(vmem_limit_bytes=56 * 2**20),
    )(aud_k, aud_q, vid_q, vid_k)


def bit_order(values):
    words = values.shape[0] // 8
    return jnp.swapaxes(values.reshape(words, 8, values.shape[1]), 0, 1).reshape(values.shape)


def word_order(values):
    words = values.shape[0] // 8
    return jnp.swapaxes(values.reshape(8, words, values.shape[1]), 0, 1).reshape(values.shape)


def pack_kernel(
    own, sums, aud_k, aud_v, aud_q, aud_g, lines, gain_k, gain_q, scales, *outs, features
):
    total = sum(sums[i] for i in range(sums.shape[0]))
    line = lax.rsqrt(total / features + EPS)
    scales[...] = line
    heads, rows, dim = aud_k.shape
    column = columns(line[:, : 2 * rows], dim)
    for i, out in enumerate(outs):
        head = jnp.bitwise_xor(own[0], i)
        k = (aud_k[head].astype(F32) * column[:rows] * gain_k[pl.ds(head, 1), :]).astype(BF16)
        out[:rows] = bit_order(k.astype(F32)).astype(BF16)
        out[rows : 2 * rows] = bit_order(aud_v[head].astype(F32)).astype(BF16)
        out[2 * rows : 3 * rows] = (
            aud_q[head].astype(F32) * column[rows:] * gain_q[pl.ds(head, 1), :]
        ).astype(BF16)
        out[3 * rows : 4 * rows] = (2.0 * aud_g[head].astype(F32)).astype(BF16)
        out[4 * rows :] = lines[head]


def pack_audio(own, sums, aud_k, aud_v, aud_q, aud_g, lines, gain_k, gain_q, features):
    heads, rows, dim = aud_k.shape
    smem, vmem = pl.BlockSpec(memory_space=pltpu.SMEM), pl.BlockSpec(memory_space=pltpu.VMEM)
    scales, *pieces = pl.pallas_call(
        functools.partial(pack_kernel, features=features),
        in_specs=[smem] + [vmem] * 8,
        out_shape=[jax.ShapeDtypeStruct((1, sums.shape[2]), F32)]
        + [jax.ShapeDtypeStruct((4 * rows + LINES, dim), BF16)] * heads,
        compiler_params=pltpu.CompilerParams(vmem_limit_bytes=24 * 2**20),
    )(own, sums, aud_k, aud_v, aud_q, aud_g, lines, gain_k, gain_q)
    return pieces, scales


def means_kernel(own, scales, aud_k, aud_q, gain_k, gain_q, vid_line, *refs):
    pieces, out = refs[:-1], refs[-1]
    heads, rows, dim = aud_k.shape
    total_k = total_q = jnp.zeros((rows, dim), F32)
    for i, piece in enumerate(pieces):
        head = jnp.bitwise_xor(own[0], i)
        up_k, up_q = word_order(piece[0].astype(F32)), piece[2].astype(F32)
        total_k += up_k * gain_k[pl.ds(head, 1), :] * aud_k[head].astype(F32)
        total_q += up_q * gain_q[pl.ds(head, 1), :] * aud_q[head].astype(F32)
    line = row_line(jnp.concatenate([total_k, total_q], axis=0)) * scales[:, : 2 * rows]
    line = jnp.concatenate([line, vid_line[...]], axis=1)
    for i in range(out.shape[0]):
        out[i] = line


def mean_lines(own, scales, aud_k, aud_q, gain_k, gain_q, vid_line, pieces):
    smem, vmem = pl.BlockSpec(memory_space=pltpu.SMEM), pl.BlockSpec(memory_space=pltpu.VMEM)
    return pl.pallas_call(
        means_kernel,
        in_specs=[smem] + [vmem] * (6 + len(pieces)),
        out_shape=jax.ShapeDtypeStruct((HEAD_GROUPS,) + scales.shape, F32),
        compiler_params=pltpu.CompilerParams(vmem_limit_bytes=24 * 2**20),
    )(own, scales, aud_k, aud_q, gain_k, gain_q, vid_line, *pieces)


def finish_kernel(own, means, scales, *refs, features):
    aud_k, aud_q, vid_q, vid_k, gain_ak, gain_aq, gain_vq, gain_vk, up_vq, up_vk = refs[:10]
    pieces = refs[10 : 10 + QUAD]
    out_ak, out_aq, out_av, out_vq, out_vk = refs[10 + QUAD :]
    heads, rows, dim = aud_k.shape
    mean_line = sum(means[i] for i in range(means.shape[0])) / features
    scale_col, mean_col = columns(scales[...], dim), columns(mean_line, dim)
    cut, more = 2 * rows, vid_q.shape[1]

    def gradient(tokens, upstream, gain, head, first, last):
        scale, mean = scale_col[first:last], mean_col[first:last]
        weighted = upstream * gain[pl.ds(head, 1), :]
        return (scale * (weighted - tokens[head].astype(F32) * scale * mean)).astype(BF16)

    for i, piece in enumerate(pieces):
        head = jnp.bitwise_xor(own[0], i)
        up_k, up_v, up_q = [piece[j].astype(F32) for j in range(3)]
        out_ak[head] = gradient(aud_k, word_order(up_k), gain_ak, head, 0, rows)
        out_aq[head] = gradient(aud_q, up_q, gain_aq, head, rows, cut)
        out_av[head] = word_order(up_v).astype(BF16)
    for i in range(heads):
        out_vq[i] = gradient(vid_q, up_vq[i].astype(F32), gain_vq, i, cut, cut + more)
        up_k = word_order(up_vk[i].astype(F32))
        out_vk[i] = gradient(vid_k, up_k, gain_vk, i, cut + more, cut + 2 * more)


def finish(own, means, scales, tokens, gains, vid_ups, pieces, features):
    shapes = [tokens[0], tokens[1], tokens[0], tokens[2], tokens[3]]
    smem, vmem = pl.BlockSpec(memory_space=pltpu.SMEM), pl.BlockSpec(memory_space=pltpu.VMEM)
    return pl.pallas_call(
        functools.partial(finish_kernel, features=features),
        in_specs=[smem] + [vmem] * (12 + len(pieces)),
        out_shape=[jax.ShapeDtypeStruct(t.shape, BF16) for t in shapes],
        compiler_params=pltpu.CompilerParams(vmem_limit_bytes=32 * 2**20),
    )(own, means, scales, *tokens, *gains, *vid_ups, *pieces)


def bundle_kernel(own, *refs):
    pieces, (out, tails) = refs[:QUAD], refs[QUAD:]
    rows = (pieces[0].shape[0] - LINES) // 4
    for i, piece in enumerate(pieces):
        place = jnp.bitwise_xor(own[0], i)
        for j in range(4):
            first = pl.multiple_of((j * QUAD + place) * rows, rows)
            out[pl.ds(first, rows)] = piece[j * rows : (j + 1) * rows]
        tails[place] = piece[4 * rows :].astype(F32)
    lines = [tails[i, :3] for i in range(QUAD)]
    lines.append(jnp.zeros((LINES - 3 * QUAD, out.shape[1]), F32))
    out[4 * QUAD * rows :] = jnp.concatenate(lines, axis=0).astype(BF16)


def plane_bundle(own, pieces):
    depth, dim = pieces[0].shape
    smem, vmem = pl.BlockSpec(memory_space=pltpu.SMEM), pl.BlockSpec(memory_space=pltpu.VMEM)
    return pl.pallas_call(
        bundle_kernel,
        in_specs=[smem] + [vmem] * QUAD,
        out_shape=jax.ShapeDtypeStruct((QUAD * (depth - LINES) + LINES, dim), BF16),
        scratch_shapes=[pltpu.VMEM((QUAD, LINES, dim), F32)],
        compiler_params=pltpu.CompilerParams(vmem_limit_bytes=24 * 2**20),
    )(own, *pieces)


def join_kernel(own, part, up, down, *homes):
    rows = homes[0].shape[1]
    for i, home in enumerate(homes):
        cut = pl.ds(pl.multiple_of(jnp.bitwise_xor(own[0], i) * rows, rows), rows)
        for j in range(home.shape[0]):
            total = part[0, j, cut] + up[j, cut].astype(F32) + down[j, cut].astype(F32)
            home[j] = total.astype(BF16)


def join_parts(own, part, up, down):
    count, rows, dim = up.shape
    return pl.pallas_call(
        join_kernel,
        grid_spec=pltpu.PrefetchScalarGridSpec(
            num_scalar_prefetch=1,
            grid=(1,),
            in_specs=[
                pl.BlockSpec((1, count, rows, dim), lambda c, s: (0, 0, 0, 0)),
                pl.BlockSpec((count, rows, dim), lambda c, s: (0, 0, 0)),
                pl.BlockSpec((count, rows, dim), lambda c, s: (0, 0, 0)),
            ],
            out_specs=[pl.BlockSpec((count, rows // QUAD, dim), lambda c, s: (0, 0, 0))] * QUAD,
        ),
        out_shape=[jax.ShapeDtypeStruct((count, rows // QUAD, dim), BF16)] * QUAD,
        compiler_params=pltpu.CompilerParams(vmem_limit_bytes=32 * 2**20),
    )(own, part, up, down)


def pack_video_kernel(
    own, scales, vid_k, vid_v, vid_q, vid_g, mask, lines, gain_k, gain_q, *outs
):
    heads, rows, dim = vid_k.shape
    first = scales.shape[1] - 2 * rows
    column_q = columns(scales[:, first : first + rows], dim)
    column_k = columns(scales[:, first + rows :], dim)
    for i, out in enumerate(outs):
        head = jnp.bitwise_xor(own[0], i)
        k = (vid_k[head].astype(F32) * column_k * gain_k[pl.ds(head, 1), :]).astype(BF16)
        out[:rows, :dim] = bit_order(k.astype(F32)).astype(BF16)
        out[:rows, dim:] = bit_order(vid_v[head].astype(F32)).astype(BF16)
        out[rows : 2 * rows, :dim] = (
            vid_q[head].astype(F32) * column_q * gain_q[pl.ds(head, 1), :]
        ).astype(BF16)
        out[rows : 2 * rows, dim:] = (2.0 * vid_g[head].astype(F32)).astype(BF16)
        out[2 * rows : 3 * rows] = mask[head].astype(F32).T.astype(BF16)
        out[3 * rows :] = lines[head]


def pack_video(own, scales, vid_k, vid_v, vid_q, vid_g, mask, lines, gain_k, gain_q):
    heads, rows, dim = vid_k.shape
    smem = pl.BlockSpec(memory_space=pltpu.SMEM)
    vmem = pl.BlockSpec(memory_space=pltpu.VMEM)
    return pl.pallas_call(
        pack_video_kernel,
        in_specs=[smem] + [vmem] * 9,
        out_shape=[jax.ShapeDtypeStruct((3 * rows + LINES, 2 * dim), BF16)] * heads,
        compiler_params=pltpu.CompilerParams(vmem_limit_bytes=24 * 2**20),
    )(own, scales, vid_k, vid_v, vid_q, vid_g, mask, lines, gain_k, gain_q)


def pack_words_kernel(own, mask, *outs):
    for i, out in enumerate(outs):
        words = mask[jnp.bitwise_xor(own[0], i)].astype(F32).astype(BF16)
        depth, wide = words.shape[0], out.shape[1]
        for j in range(words.shape[1] // wide):
            out[j * depth : (j + 1) * depth] = words[:, j * wide : (j + 1) * wide]


def pack_words(own, mask, wide):
    heads, depth, queries = mask.shape
    return pl.pallas_call(
        pack_words_kernel,
        in_specs=[pl.BlockSpec(memory_space=pltpu.SMEM), pl.BlockSpec(memory_space=pltpu.VMEM)],
        out_shape=[jax.ShapeDtypeStruct((depth * queries // wide, wide), BF16)] * heads,
        compiler_params=pltpu.CompilerParams(vmem_limit_bytes=24 * 2**20),
    )(own, mask)


def words_first(rows):
    split = rows.reshape(rows.shape[:-2] + (8, rows.shape[-2] // 8, rows.shape[-1]))
    return jnp.swapaxes(split, -3, -2).reshape(rows.shape)


def to_quad(rows):
    return lax.all_to_all(rows, QUAD_AXES, 0, 0, tiled=True)


def shift(rows, step):
    return lax.ppermute(rows, "plane", [(i, (i + step) % PLANES) for i in range(PLANES)])


def after(value, *others):
    return lax.optimization_barrier((value,) + others)[0]


def token_sums(tokens, scales, gain_rows, upstream):
    weighted = upstream.astype(F32) * gain_rows[:, None, :]
    return jnp.sum(weighted * (tokens.astype(F32) * scales[None, :, None]), axis=(0, 2))


def local(
    vid_query, vid_key, vid_value, vid_out, vid_grad, vid_lse, vid_mask,
    aud_query, aud_key, aud_value, aud_out, aud_grad, aud_lse, aud_mask,
    gain_vq, gain_ak, gain_aq, gain_vk,
):
    heads, vid_rows, dim = vid_query.shape
    aud_rows = aud_query.shape[1]
    plane_rows = QUAD * aud_rows
    feature_count = HEAD_GROUPS * heads * dim
    scale = dim**-0.5
    own_plane = lax.axis_index("plane")
    own = lax.axis_index(QUAD_AXES)

    own_line = own.astype(jnp.int32).reshape(1)

    sums = head_sums(aud_key, aud_query, vid_query, vid_key)
    arrived = from_heads(sums)

    def lines(lse, out, grad):
        delta = jnp.sum(grad.astype(F32) * out.astype(F32), axis=2)
        rest, found = jnp.stack([lse * LOG2E, delta], axis=1), []
        for _ in range(3):
            found.append(lax.reduce_precision(rest, 8, 7))
            rest = rest - found[-1]
        return jnp.stack(found, axis=1).astype(BF16)

    aud_lines = jnp.pad(
        lines(aud_lse, aud_out, aud_grad).reshape(heads, -1, dim),
        ((0, 0), (0, LINES - 6 * aud_rows // dim), (0, 0)),
    )
    vid_lines = jnp.pad(
        lines(vid_lse, vid_out, vid_grad).reshape(heads, 6, vid_rows),
        ((0, 0), (0, LINES - 6), (0, 0)),
    )

    def across_quad(pieces):
        return [pieces[0]] + [
            lax.ppermute(pieces[offset], QUAD_AXES, [(i, i ^ offset) for i in range(QUAD)])
            for offset in range(1, QUAD)
        ]

    words = pack_words(after(own_line, sums), jnp.swapaxes(aud_mask, 1, 2), plane_rows)
    words = across_quad(words)

    audio, scales = pack_audio(
        own_line, arrived, aud_key, aud_value, aud_query, aud_grad, aud_lines, gain_ak, gain_aq, feature_count
    )
    video = across_quad(
        pack_video(
            after(own_line, audio[0]), scales, vid_key, vid_value, vid_query, vid_grad, vid_mask,
            vid_lines, gain_vk, gain_vq,
        )
    )
    mine = plane_bundle(own_line, across_quad(after(audio, *words[1:])))
    below, above = [mine, shift(mine, 1)], [mine, shift(mine, -1)]
    def plane_ids(*offsets):
        return jnp.stack([own.astype(jnp.int32)] + [(own_plane + o) % PLANES for o in offsets]).astype(jnp.int32)

    below.append(shift(below[1], 1))
    above.append(shift(above[1], -1))
    part_near, total = attention(
        plane_ids(0, -1, 1), [(mine,), (below[1],), (above[1],)], words, video, None, False, scale
    )
    below.append(shift(below[2], 1))
    above.append(shift(above[2], -1))
    part_2, total = attention(
        plane_ids(-2, 2), [(below[2],), (above[2],)], words, video, total, False, scale
    )
    half = 2 * plane_rows
    far_kv, far_qg = shift(below[3][:half], 1), shift(above[3][half:], -1)
    part_3, total = attention(
        plane_ids(-3, 3), [(below[3],), (above[3],)], words, video, total, False, scale
    )
    half_rows = plane_rows // 2
    part_far, vid_parts = attention(
        plane_ids(4), [(far_kv, far_qg)], words, video, total, True, scale
    )
    part_far = part_far[0].astype(BF16)
    up, more = shift(part_far[:, :half_rows], 1), shift(part_far[:, half_rows:], -1)

    def onward(part, arrived, step):
        return shift((part + arrived.astype(F32)).astype(BF16), step)

    up_sum = jnp.concatenate([part_3[1, :, :half_rows] + up.astype(F32), part_3[1, :, half_rows:]], axis=1)
    down_sum = jnp.concatenate([part_3[0, :, :half_rows], part_3[0, :, half_rows:] + more.astype(F32)], axis=1)
    up, down = shift(up_sum.astype(BF16), 1), shift(down_sum.astype(BF16), -1)
    up, down = onward(part_2[1], up, 1), onward(part_2[0], down, -1)
    up, down = onward(part_near[2], up, 1), onward(part_near[1], down, -1)
    home = join_parts(own_line, part_near, up, down)

    cuts = (aud_rows, 2 * aud_rows, 2 * aud_rows + vid_rows)
    scale_ak, scale_aq, scale_vq, scale_vk = jnp.split(scales[0], cuts)
    up_vk, grad_vv, up_vq = jnp.swapaxes(to_quad(vid_parts), 0, 1)
    grad_vv = words_first(grad_vv)
    local_vq = token_sums(vid_query, scale_vq, gain_vq, up_vq)
    local_vk = token_sums(vid_key, scale_vk, gain_vk, words_first(up_vk))

    pieces = across_quad(home)
    vid_line = jnp.concatenate([local_vq, local_vk])[None]
    means = mean_lines(own_line, scales, aud_key, aud_query, gain_ak, gain_aq, vid_line, pieces)
    grad_ak, grad_aq, grad_av, grad_vq, grad_vk = finish(
        own_line, from_heads(means), scales, (aud_key, aud_query, vid_query, vid_key),
        (gain_ak, gain_aq, gain_vq, gain_vk), (up_vq, up_vk), pieces, feature_count,
    )
    return grad_vq, grad_vk, grad_vv, grad_aq, grad_ak, grad_av


def solution(mesh):
    fine = Mesh(
        mesh.devices.reshape(PLANES, NEAR, CORES, HEAD_GROUPS), ("plane", "near", "core", "head")
    )
    rows, lines, gain = P("head", CTX_AXES, None), P("head", CTX_AXES), P("head", None)
    return jax.shard_map(
        local,
        mesh=fine,
        in_specs=(rows,) * 5 + (lines, rows) + (rows,) * 5 + (lines, P("head", None, CTX_AXES)) + (gain,) * 4,
        out_specs=(rows,) * 6,
        check_vma=False,
    )
```

```python
import functools
import math

import jax
import jax.numpy as jnp
from jax import lax
from jax.experimental import pallas as pl
from jax.experimental.pallas import tpu as pltpu
from jax.sharding import Mesh
from jax.sharding import PartitionSpec as P

EPS = 1e-06
LOG2E = math.log2(math.e)
F32 = jnp.float32
BF16 = jnp.bfloat16
PLANES, NEAR, CORES, HEAD_GROUPS = 8, 2, 2, 8
QUAD = NEAR * CORES
LINES = 16
QUAD_AXES = ("near", "core")
CTX_AXES = ("plane", "near", "core")


def dot_nt(left, right):
    return lax.dot_general(left, right, (((1,), (1,)), ((), ())), preferred_element_type=F32)


def dot_nn(left, right):
    return lax.dot_general(left, right, (((1,), (0,)), ((), ())), preferred_element_type=F32)


def dot_tn(left, right):
    return lax.dot_general(left, right, (((0,), (0,)), ((), ())), preferred_element_type=F32)


def keep_rows(words, group):
    wide = words.astype(F32).astype(jnp.int32)
    picked = [
        jnp.bitwise_and(wide[first : first + group], 1 << bit)
        for first in range(0, words.shape[0], group)
        for bit in range(8)
    ]
    return jnp.concatenate(picked, axis=0) != 0


def probs_and_scores(keys, values, queries, twice_grad, lse2, delta, kept, coefficient):
    probs = jnp.exp2(dot_nt(keys, queries) * coefficient - lse2)
    dropped = jnp.where(kept, probs, 0.0).astype(BF16)
    prob_grad = jnp.where(kept, dot_nt(values, twice_grad), 0.0)
    return dropped, (probs * (prob_grad - delta)).astype(BF16)


def attention_kernel(ids, *refs, scale, count, first, last):
    coefficient = scale * LOG2E
    pieces = QUAD
    refs = list(refs)

    def take(number):
        taken, refs[:number] = refs[:number], []
        return taken

    per_plane = [(take(1)[0], take(1)[0], take(pieces), take(pieces)) for _ in range(count)]
    vid_kv, vid_qg, vid_small = take(pieces), take(pieces), take(pieces)
    if not first:
        sums_in, refs = refs[0], refs[1:]
    aud_out, vid_out = refs[:2]
    own = ids[0]
    rows, wide = vid_kv[0].shape
    dim = wide // 2

    def joined(blocks, axis=0):
        return jnp.concatenate([block[...] for block in blocks], axis=axis)

    both = joined(vid_kv)
    k_v, v_v = both[:, :dim], both[:, dim:]
    both = joined(vid_qg)
    q_v, g_v = both[:, :dim], both[:, dim:]
    small = joined(vid_small, 1).astype(F32)
    small = small[0:2] + small[2:4] + small[4:6]
    lse_v, delta_v = small[0:1], small[1:2]
    sums = [jnp.zeros((pieces * rows, dim), F32) if first else sums_in[i] for i in range(3)]
    for i, (aud_kv, aud_qg, words_v, words_a) in enumerate(per_plane):
        k_a, v_a = aud_kv[:rows], aud_kv[rows : 2 * rows]
        q_a, g_a = aud_qg[:rows], aud_qg[rows : 2 * rows]
        small = aud_qg[2 * rows :].astype(F32)
        small = [small[j : j + 1] + small[j + 1 : j + 2] + small[j + 2 : j + 3] for j in range(0, 12, 3)]
        turned = [pltpu.roll(values, dim // 2, 1) for values in small]
        left = lax.broadcasted_iota(jnp.int32, (1, dim), 1) < dim // 2
        lse_a = [jnp.where(left, small[j], turned[j + 1]) for j in (0, 2)]
        delta_a = [jnp.where(left, turned[j], small[j + 1]) for j in (0, 2)]
        lse_a, delta_a = jnp.concatenate(lse_a, axis=1), jnp.concatenate(delta_a, axis=1)
        kept = keep_rows(joined(words_v, 1), 8)
        dropped, score_grad = probs_and_scores(
            k_a, v_a, q_v, g_v, lse_v, delta_v, kept, coefficient
        )
        aud_out[i, 0] = dot_nn(score_grad, q_v) * scale
        aud_out[i, 1] = dot_nn(dropped, g_v)
        sums[2] = sums[2] + dot_tn(score_grad, k_a)
        kept = keep_rows(joined(words_a), rows // 8)
        dropped, score_grad = probs_and_scores(
            k_v, v_v, q_a, g_a, lse_a, delta_a, kept, coefficient
        )
        sums[1] = sums[1] + dot_nn(dropped, g_a)
        sums[0] = sums[0] + dot_nn(score_grad, q_a)
        aud_out[i, 2] = dot_tn(score_grad, k_v) * scale
    if last:
        sums = [sums[0] * scale, sums[1], sums[2] * scale]
        for i in range(pieces):
            for j in range(3):
                vid_out[jnp.bitwise_xor(own, i), j] = sums[j][i * rows : (i + 1) * rows].astype(BF16)
    else:
        for j in range(3):
            vid_out[j] = sums[j]


def attention(ids, planes, words, video, sums, last, scale):
    count, first = len(planes), sums is None
    pieces, wide = len(video), video[0].shape[1]
    dim, rows = wide // 2, wide
    plane_words, vid_count = rows // 8, pieces * rows
    specs, operands = [], []

    def add(array, shape, index):
        operands.append(array)
        specs.append(pl.BlockSpec(shape, index))

    for i, halves in enumerate(planes):
        if len(halves) == 1:
            add(halves[0], (2 * rows, dim), lambda c, s: (0, 0))
            add(halves[0], (pl.Element(2 * rows + LINES), pl.Element(dim)), lambda c, s: (2 * rows, 0))
        else:
            for half in halves:
                add(half, half.shape, lambda c, s: (0, 0))
        for piece in video:
            add(piece, (plane_words, wide), lambda c, s, i=i: (2 * rows // plane_words + s[1 + i], 0))
        for piece in words:
            add(piece, (plane_words, wide), lambda c, s, i=i: (s[1 + i], 0))
    for depth, place in ((rows, 0), (rows, 1), (LINES, 3 * rows // LINES)):
        for piece in video:
            add(piece, (depth, wide), lambda c, s, place=place: (place, 0))
    if not first:
        add(sums, sums.shape, lambda c, s: (0, 0, 0))
    if last:
        vid_shape, vid_type = (pieces, 3, rows, dim), BF16
    else:
        vid_shape, vid_type = (3, vid_count, dim), F32
    pairs = 2 * count * rows * vid_count
    return pl.pallas_call(
        functools.partial(attention_kernel, scale=scale, count=count, first=first, last=last),
        grid_spec=pltpu.PrefetchScalarGridSpec(
            num_scalar_prefetch=1,
            grid=(1,),
            in_specs=specs,
            out_specs=[
                pl.BlockSpec((count, 3, rows, dim), lambda c, s: (0, 0, 0, 0)),
                pl.BlockSpec(vid_shape, lambda c, s: (0,) * len(vid_shape)),
            ],
        ),
        out_shape=[
            jax.ShapeDtypeStruct((count, 3, rows, dim), F32),
            jax.ShapeDtypeStruct(vid_shape, vid_type),
        ],
        compiler_params=pltpu.CompilerParams(vmem_limit_bytes=32 * 2**20),
        cost_estimate=pl.CostEstimate(
            flops=10 * pairs * dim, bytes_accessed=4 * 2**20, transcendentals=pairs
        ),
    )(ids, *operands)


def from_heads(lines):
    return lax.all_to_all(lines, "head", 0, 0, tiled=True)


def row_line(values):
    return jnp.sum(values.T, axis=0, keepdims=True)


def columns(line, dim):
    return jnp.broadcast_to(line, (dim, line.shape[1])).T


def sums_kernel(aud_k, aud_q, vid_q, vid_k, out):
    lines = []
    pair = []
    for tokens in (aud_k, aud_q, vid_q, vid_k):
        total = 0.0
        for i in range(tokens.shape[0]):
            values = tokens[i].astype(F32)
            total = total + values * values
        pair.append(total)
    both = jnp.concatenate(pair[:2], axis=0)
    line = jnp.concatenate([row_line(both), row_line(pair[2]), row_line(pair[3])], axis=1)
    for i in range(out.shape[0]):
        out[i] = line


def head_sums(aud_k, aud_q, vid_q, vid_k):
    rows = 2 * (aud_k.shape[1] + vid_k.shape[1])
    return pl.pallas_call(
        sums_kernel,
        out_shape=jax.ShapeDtypeStruct((HEAD_GROUPS, 1, rows), F32),
        compiler_params=pltpu.CompilerParams(vmem_limit_bytes=56 * 2**20),
    )(aud_k, aud_q, vid_q, vid_k)


def bit_order(values):
    words = values.shape[0] // 8
    return jnp.swapaxes(values.reshape(words, 8, values.shape[1]), 0, 1).reshape(values.shape)


def word_order(values):
    words = values.shape[0] // 8
    return jnp.swapaxes(values.reshape(8, words, values.shape[1]), 0, 1).reshape(values.shape)


def pack_kernel(sums, aud_k, aud_v, aud_q, aud_g, lines, gain_k, gain_q, out, scales, *, features):
    total = sum(sums[i] for i in range(sums.shape[0]))
    line = lax.rsqrt(total / features + EPS)
    scales[...] = line
    heads, rows, dim = aud_k.shape
    column = columns(line[:, : 2 * rows], dim)
    for i in range(heads):
        k = (aud_k[i].astype(F32) * column[:rows] * gain_k[i : i + 1]).astype(BF16)
        out[i, :rows] = bit_order(k.astype(F32)).astype(BF16)
        out[i, rows : 2 * rows] = bit_order(aud_v[i].astype(F32)).astype(BF16)
        out[i, 2 * rows : 3 * rows] = (
            aud_q[i].astype(F32) * column[rows:] * gain_q[i : i + 1]
        ).astype(BF16)
        out[i, 3 * rows : 4 * rows] = (2.0 * aud_g[i].astype(F32)).astype(BF16)
        out[i, 4 * rows :] = lines[i]


def pack_audio(sums, aud_k, aud_v, aud_q, aud_g, lines, gain_k, gain_q, features):
    heads, rows, dim = aud_k.shape
    return pl.pallas_call(
        functools.partial(pack_kernel, features=features),
        out_shape=[
            jax.ShapeDtypeStruct((heads, 4 * rows + LINES, dim), BF16),
            jax.ShapeDtypeStruct((1, sums.shape[2]), F32),
        ],
        compiler_params=pltpu.CompilerParams(vmem_limit_bytes=24 * 2**20),
    )(sums, aud_k, aud_v, aud_q, aud_g, lines, gain_k, gain_q)


def means_kernel(own, scales, aud_k, aud_q, gain_k, gain_q, vid_line, *refs):
    pieces, out = refs[:-1], refs[-1]
    heads, rows, dim = aud_k.shape
    total_k = total_q = jnp.zeros((rows, dim), F32)
    for i, piece in enumerate(pieces):
        head = jnp.bitwise_xor(own[0], i)
        up_k, up_q = word_order(piece[0].astype(F32)), piece[2].astype(F32)
        total_k += up_k * gain_k[pl.ds(head, 1), :] * aud_k[head].astype(F32)
        total_q += up_q * gain_q[pl.ds(head, 1), :] * aud_q[head].astype(F32)
    line = row_line(jnp.concatenate([total_k, total_q], axis=0)) * scales[:, : 2 * rows]
    line = jnp.concatenate([line, vid_line[...]], axis=1)
    for i in range(out.shape[0]):
        out[i] = line


def mean_lines(own, scales, aud_k, aud_q, gain_k, gain_q, vid_line, pieces):
    smem, vmem = pl.BlockSpec(memory_space=pltpu.SMEM), pl.BlockSpec(memory_space=pltpu.VMEM)
    return pl.pallas_call(
        means_kernel,
        in_specs=[smem] + [vmem] * (6 + len(pieces)),
        out_shape=jax.ShapeDtypeStruct((HEAD_GROUPS,) + scales.shape, F32),
        compiler_params=pltpu.CompilerParams(vmem_limit_bytes=24 * 2**20),
    )(own, scales, aud_k, aud_q, gain_k, gain_q, vid_line, *pieces)


def finish_kernel(own, means, scales, *refs, features):
    aud_k, aud_q, vid_q, vid_k, gain_ak, gain_aq, gain_vq, gain_vk, up_vq, up_vk = refs[:10]
    pieces = refs[10 : 10 + QUAD]
    out_ak, out_aq, out_av, out_vq, out_vk = refs[10 + QUAD :]
    heads, rows, dim = aud_k.shape
    mean_line = sum(means[i] for i in range(means.shape[0])) / features
    scale_col, mean_col = columns(scales[...], dim), columns(mean_line, dim)
    cut, more = 2 * rows, vid_q.shape[1]

    def gradient(tokens, upstream, gain, head, first, last):
        scale, mean = scale_col[first:last], mean_col[first:last]
        weighted = upstream * gain[pl.ds(head, 1), :]
        return (scale * (weighted - tokens[head].astype(F32) * scale * mean)).astype(BF16)

    for i, piece in enumerate(pieces):
        head = jnp.bitwise_xor(own[0], i)
        up_k, up_v, up_q = [piece[j].astype(F32) for j in range(3)]
        out_ak[head] = gradient(aud_k, word_order(up_k), gain_ak, head, 0, rows)
        out_aq[head] = gradient(aud_q, up_q, gain_aq, head, rows, cut)
        out_av[head] = word_order(up_v).astype(BF16)
    for i in range(heads):
        out_vq[i] = gradient(vid_q, up_vq[i].astype(F32), gain_vq, i, cut, cut + more)
        up_k = word_order(up_vk[i].astype(F32))
        out_vk[i] = gradient(vid_k, up_k, gain_vk, i, cut + more, cut + 2 * more)


def finish(own, means, scales, tokens, gains, vid_ups, pieces, features):
    shapes = [tokens[0], tokens[1], tokens[0], tokens[2], tokens[3]]
    smem, vmem = pl.BlockSpec(memory_space=pltpu.SMEM), pl.BlockSpec(memory_space=pltpu.VMEM)
    return pl.pallas_call(
        functools.partial(finish_kernel, features=features),
        in_specs=[smem] + [vmem] * (12 + len(pieces)),
        out_shape=[jax.ShapeDtypeStruct(t.shape, BF16) for t in shapes],
        compiler_params=pltpu.CompilerParams(vmem_limit_bytes=32 * 2**20),
    )(own, means, scales, *tokens, *gains, *vid_ups, *pieces)


def bundle_kernel(audio, out):
    rows = (audio.shape[1] - LINES) // 4
    for i in range(4):
        for j in range(QUAD):
            out[pl.ds((i * QUAD + j) * rows, rows)] = audio[j, pl.ds(i * rows, rows)]
    tails = [audio[j, pl.ds(4 * rows, LINES)].astype(F32)[:3] for j in range(QUAD)]
    tails.append(jnp.zeros((LINES - 3 * QUAD, audio.shape[2]), F32))
    out[pl.ds(4 * QUAD * rows, LINES)] = jnp.concatenate(tails, axis=0).astype(BF16)


def plane_bundle(audio):
    rows, dim = (audio.shape[1] - LINES) // 4, audio.shape[2]
    return pl.pallas_call(
        bundle_kernel,
        out_shape=jax.ShapeDtypeStruct((4 * QUAD * rows + LINES, dim), BF16),
        compiler_params=pltpu.CompilerParams(vmem_limit_bytes=24 * 2**20),
    )(audio)


def join_kernel(own, part, up, down, *homes):
    rows = homes[0].shape[1]
    for i, home in enumerate(homes):
        cut = pl.ds(pl.multiple_of(jnp.bitwise_xor(own[0], i) * rows, rows), rows)
        for j in range(home.shape[0]):
            total = part[0, j, cut] + up[j, cut].astype(F32) + down[j, cut].astype(F32)
            home[j] = total.astype(BF16)


def join_parts(own, part, up, down):
    count, rows, dim = up.shape
    return pl.pallas_call(
        join_kernel,
        grid_spec=pltpu.PrefetchScalarGridSpec(
            num_scalar_prefetch=1,
            grid=(1,),
            in_specs=[
                pl.BlockSpec((1, count, rows, dim), lambda c, s: (0, 0, 0, 0)),
                pl.BlockSpec((count, rows, dim), lambda c, s: (0, 0, 0)),
                pl.BlockSpec((count, rows, dim), lambda c, s: (0, 0, 0)),
            ],
            out_specs=[pl.BlockSpec((count, rows // QUAD, dim), lambda c, s: (0, 0, 0))] * QUAD,
        ),
        out_shape=[jax.ShapeDtypeStruct((count, rows // QUAD, dim), BF16)] * QUAD,
        compiler_params=pltpu.CompilerParams(vmem_limit_bytes=32 * 2**20),
    )(own, part, up, down)


def pack_video_kernel(
    own, scales, vid_k, vid_v, vid_q, vid_g, mask, lines, gain_k, gain_q, *outs
):
    heads, rows, dim = vid_k.shape
    first = scales.shape[1] - 2 * rows
    column_q = columns(scales[:, first : first + rows], dim)
    column_k = columns(scales[:, first + rows :], dim)
    for i, out in enumerate(outs):
        head = jnp.bitwise_xor(own[0], i)
        k = (vid_k[head].astype(F32) * column_k * gain_k[pl.ds(head, 1), :]).astype(BF16)
        out[:rows, :dim] = bit_order(k.astype(F32)).astype(BF16)
        out[:rows, dim:] = bit_order(vid_v[head].astype(F32)).astype(BF16)
        out[rows : 2 * rows, :dim] = (
            vid_q[head].astype(F32) * column_q * gain_q[pl.ds(head, 1), :]
        ).astype(BF16)
        out[rows : 2 * rows, dim:] = (2.0 * vid_g[head].astype(F32)).astype(BF16)
        out[2 * rows : 3 * rows] = mask[head].astype(F32).T.astype(BF16)
        out[3 * rows :] = lines[head]


def pack_video(own, scales, vid_k, vid_v, vid_q, vid_g, mask, lines, gain_k, gain_q):
    heads, rows, dim = vid_k.shape
    smem = pl.BlockSpec(memory_space=pltpu.SMEM)
    vmem = pl.BlockSpec(memory_space=pltpu.VMEM)
    return pl.pallas_call(
        pack_video_kernel,
        in_specs=[smem] + [vmem] * 9,
        out_shape=[jax.ShapeDtypeStruct((3 * rows + LINES, 2 * dim), BF16)] * heads,
        compiler_params=pltpu.CompilerParams(vmem_limit_bytes=24 * 2**20),
    )(own, scales, vid_k, vid_v, vid_q, vid_g, mask, lines, gain_k, gain_q)


def pack_words_kernel(own, mask, *outs):
    for i, out in enumerate(outs):
        words = mask[jnp.bitwise_xor(own[0], i)].astype(F32).astype(BF16)
        depth, wide = words.shape[0], out.shape[1]
        for j in range(words.shape[1] // wide):
            out[j * depth : (j + 1) * depth] = words[:, j * wide : (j + 1) * wide]


def pack_words(own, mask, wide):
    heads, depth, queries = mask.shape
    return pl.pallas_call(
        pack_words_kernel,
        in_specs=[pl.BlockSpec(memory_space=pltpu.SMEM), pl.BlockSpec(memory_space=pltpu.VMEM)],
        out_shape=[jax.ShapeDtypeStruct((depth * queries // wide, wide), BF16)] * heads,
        compiler_params=pltpu.CompilerParams(vmem_limit_bytes=24 * 2**20),
    )(own, mask)


def words_first(rows):
    split = rows.reshape(rows.shape[:-2] + (8, rows.shape[-2] // 8, rows.shape[-1]))
    return jnp.swapaxes(split, -3, -2).reshape(rows.shape)


def to_quad(rows):
    return lax.all_to_all(rows, QUAD_AXES, 0, 0, tiled=True)


def shift(rows, step):
    return lax.ppermute(rows, "plane", [(i, (i + step) % PLANES) for i in range(PLANES)])


def after(value, *others):
    return lax.optimization_barrier((value,) + others)[0]


def token_sums(tokens, scales, gain_rows, upstream):
    weighted = upstream.astype(F32) * gain_rows[:, None, :]
    return jnp.sum(weighted * (tokens.astype(F32) * scales[None, :, None]), axis=(0, 2))


def local(
    vid_query, vid_key, vid_value, vid_out, vid_grad, vid_lse, vid_mask,
    aud_query, aud_key, aud_value, aud_out, aud_grad, aud_lse, aud_mask,
    gain_vq, gain_ak, gain_aq, gain_vk,
):
    heads, vid_rows, dim = vid_query.shape
    aud_rows = aud_query.shape[1]
    plane_rows = QUAD * aud_rows
    feature_count = HEAD_GROUPS * heads * dim
    scale = dim**-0.5
    own_plane = lax.axis_index("plane")
    own = lax.axis_index(QUAD_AXES)

    own_line = own.astype(jnp.int32).reshape(1)

    sums = head_sums(aud_key, aud_query, vid_query, vid_key)
    arrived = from_heads(sums)

    def lines(lse, out, grad):
        delta = jnp.sum(grad.astype(F32) * out.astype(F32), axis=2)
        rest, found = jnp.stack([lse * LOG2E, delta], axis=1), []
        for _ in range(3):
            found.append(lax.reduce_precision(rest, 8, 7))
            rest = rest - found[-1]
        return jnp.stack(found, axis=1).astype(BF16)

    aud_lines = jnp.pad(
        lines(aud_lse, aud_out, aud_grad).reshape(heads, -1, dim),
        ((0, 0), (0, LINES - 6 * aud_rows // dim), (0, 0)),
    )
    vid_lines = jnp.pad(
        lines(vid_lse, vid_out, vid_grad).reshape(heads, 6, vid_rows),
        ((0, 0), (0, LINES - 6), (0, 0)),
    )

    def across_quad(pieces):
        return [pieces[0]] + [
            lax.ppermute(pieces[offset], QUAD_AXES, [(i, i ^ offset) for i in range(QUAD)])
            for offset in range(1, QUAD)
        ]

    words = pack_words(after(own_line, sums), jnp.swapaxes(aud_mask, 1, 2), plane_rows)
    words = across_quad(words)

    audio, scales = pack_audio(
        arrived, aud_key, aud_value, aud_query, aud_grad, aud_lines, gain_ak, gain_aq, feature_count
    )
    video = across_quad(
        pack_video(
            after(own_line, audio), scales, vid_key, vid_value, vid_query, vid_grad, vid_mask,
            vid_lines, gain_vk, gain_vq,
        )
    )
    mine = plane_bundle(to_quad(after(audio, *words[1:])))
    below, above = [mine, shift(mine, 1)], [mine, shift(mine, -1)]
    def plane_ids(*offsets):
        return jnp.stack([own.astype(jnp.int32)] + [(own_plane + o) % PLANES for o in offsets]).astype(jnp.int32)

    below.append(shift(below[1], 1))
    above.append(shift(above[1], -1))
    part_near, total = attention(
        plane_ids(0, -1, 1), [(mine,), (below[1],), (above[1],)], words, video, None, False, scale
    )
    below.append(shift(below[2], 1))
    above.append(shift(above[2], -1))
    part_2, total = attention(
        plane_ids(-2, 2), [(below[2],), (above[2],)], words, video, total, False, scale
    )
    half = 2 * plane_rows
    far_kv, far_qg = shift(below[3][:half], 1), shift(above[3][half:], -1)
    part_3, total = attention(
        plane_ids(-3, 3), [(below[3],), (above[3],)], words, video, total, False, scale
    )
    half_rows = plane_rows // 2
    part_far, vid_parts = attention(
        plane_ids(4), [(far_kv, far_qg)], words, video, total, True, scale
    )
    part_far = part_far[0].astype(BF16)
    up, more = shift(part_far[:, :half_rows], 1), shift(part_far[:, half_rows:], -1)

    def onward(part, arrived, step):
        return shift((part + arrived.astype(F32)).astype(BF16), step)

    up_sum = jnp.concatenate([part_3[1, :, :half_rows] + up.astype(F32), part_3[1, :, half_rows:]], axis=1)
    down_sum = jnp.concatenate([part_3[0, :, :half_rows], part_3[0, :, half_rows:] + more.astype(F32)], axis=1)
    up, down = shift(up_sum.astype(BF16), 1), shift(down_sum.astype(BF16), -1)
    up, down = onward(part_2[1], up, 1), onward(part_2[0], down, -1)
    up, down = onward(part_near[2], up, 1), onward(part_near[1], down, -1)
    home = join_parts(own_line, part_near, up, down)

    cuts = (aud_rows, 2 * aud_rows, 2 * aud_rows + vid_rows)
    scale_ak, scale_aq, scale_vq, scale_vk = jnp.split(scales[0], cuts)
    up_vk, grad_vv, up_vq = jnp.swapaxes(to_quad(vid_parts), 0, 1)
    grad_vv = words_first(grad_vv)
    local_vq = token_sums(vid_query, scale_vq, gain_vq, up_vq)
    local_vk = token_sums(vid_key, scale_vk, gain_vk, words_first(up_vk))

    pieces = across_quad(home)
    vid_line = jnp.concatenate([local_vq, local_vk])[None]
    means = mean_lines(own_line, scales, aud_key, aud_query, gain_ak, gain_aq, vid_line, pieces)
    grad_ak, grad_aq, grad_av, grad_vq, grad_vk = finish(
        own_line, from_heads(means), scales, (aud_key, aud_query, vid_query, vid_key),
        (gain_ak, gain_aq, gain_vq, gain_vk), (up_vq, up_vk), pieces, feature_count,
    )
    return grad_vq, grad_vk, grad_vv, grad_aq, grad_ak, grad_av


def solution(mesh):
    fine = Mesh(
        mesh.devices.reshape(PLANES, NEAR, CORES, HEAD_GROUPS), ("plane", "near", "core", "head")
    )
    rows, lines, gain = P("head", CTX_AXES, None), P("head", CTX_AXES), P("head", None)
    return jax.shard_map(
        local,
        mesh=fine,
        in_specs=(rows,) * 5 + (lines, rows) + (rows,) * 5 + (lines, P("head", None, CTX_AXES)) + (gain,) * 4,
        out_specs=(rows,) * 6,
        check_vma=False,
    )
```
